512 devices in a mesh: panel: 2 (over z_hi), lat: 8 (over y), lon: 32 (over x, z_lo, core).
Axes of the slice: x: 4, y: 8, z: 8 (z_hi: 2, z_lo: 4; z = z_hi * 4 + z_lo), core: 2. Of those that a mesh axis runs over, the one named last changes fastest.
Arguments:
- viscosity: float32 [2, 64, 512, 128], P('panel', 'lat', 'lon'), may hold values from 0.001 to 1000, as said below
- forcing: float32 [4, 2, 64, 512, 128], P(None, 'panel', 'lat', 'lon'), may hold values from -6 to 6
- send_cell: int32 [2, 8, 32, 1024], P('panel', 'lat', 'lon'), may hold values from 0 to 127, as said below
- partner: int32 [2, 8, 32, 4], P('panel', 'lat', 'lon'), may hold values from 0 to 255, as said below
- ghost_src: int32 [2, 8, 32, 48], P('panel', 'lat', 'lon'), may hold values from 0 to 3
- ghost_weight: float32 [2, 8, 32, 48, 4], P('panel', 'lat', 'lon'), may hold values from 0.05 to 1
- ghost_angle: float32 [2, 8, 32, 48], P('panel', 'lat', 'lon'), may hold values from -3.140625 to 3.140625
Outputs:
- state: float32 [4, 2, 64, 512, 128], P(None, 'panel', 'lat', 'lon')
The draws below stay inside these ranges and needn't reach their ends.
Inputs may be any that keep to these rules, and one draw needn't show every extreme that they name: `send_cell`: for each destination, the 4 slots name the cells (r, c), (r, c + 1), (r + 1, c), (r + 1, c + 1) of this device's block, in that order, numbered r * 16 + c. `partner`: the four partners form a 2 by 2 block of adjacent devices: b, b + 1, b + 32, b + 32 + 1 in the numbering lat * 32 + lon, in that order. viscosity varies over the shell with sharp radial interfaces.
All inputs are finite; a program needn't handle non-finite values.
Results may differ from the reference program's by a relative error of at most 0.0001.
Values sent between devices are 32-bit elements; how exact they have to be, the bound alone decides.
A program may use at most 64 MiB of HBM per device.

```python
import math
import jax
import jax.numpy as jnp
from jax import lax

CTH = 8
CPH = 16
NR = 128
CAP = 4
ITERS = 3
NTH = 64
NPH = 512
GH = 48
SENDS = 1024
N_PANEL = 2
N_LAT = 8
N_LON = 32


def draw_viscosity(key, part):
    key = jax.random.fold_in(key, 3)
    keys = jax.random.split(key, 3)
    theta = ((jnp.arange(NTH, dtype=jnp.float32) + 0.5) / NTH)[None, :, None, None]
    phi = ((jnp.arange(NPH, dtype=jnp.float32) + 0.5) / NPH)[None, None, :, None]
    depth = ((jnp.arange(NR, dtype=jnp.float32) + 0.5) / NR)[None, None, None, :]
    phases = jax.random.uniform(keys[0], (N_PANEL, 3), minval=0.0, maxval=2.0 * math.pi)
    freq = jax.random.randint(keys[1], (N_PANEL, 2), 1, 3).astype(jnp.float32)
    ph0 = phases[:, 0][:, None, None, None]
    ph1 = phases[:, 1][:, None, None, None]
    ph2 = phases[:, 2][:, None, None, None]
    fr0 = freq[:, 0][:, None, None, None]
    fr1 = freq[:, 1][:, None, None, None]
    smooth = 1.3 * jnp.sin(2.0 * math.pi * fr0 * phi + ph0) * jnp.cos(math.pi * theta + ph1)
    smooth = smooth + 0.8 * jnp.sin(2.0 * math.pi * fr1 * depth + ph2)
    level = 2.6 * jnp.tanh(smooth)
    level = level + jnp.where(depth > 0.85, 0.8, 0.0)
    rough = jax.random.uniform(keys[2], (N_PANEL, NTH, NPH, NR), minval=-0.3, maxval=0.3)
    level = jnp.clip(level + rough, -3.0, 3.0)
    return jnp.power(10.0, level).astype(jnp.float32)


def draw_send_cell(key, part):
    key = jax.random.fold_in(key, 7)
    keys = jax.random.split(key, 3)
    shape = (N_PANEL, N_LAT, N_LON, N_LAT * N_LON)
    row0 = jax.random.randint(keys[0], shape, 0, CTH - 1)
    col0 = jax.random.randint(keys[1], shape, 0, CPH - 1)
    flat = jnp.arange(N_PANEL * N_LAT * N_LON * N_LAT * N_LON, dtype=jnp.int32).reshape(shape)
    chosen = jax.random.randint(keys[2], (), 0, N_PANEL * N_LAT * N_LON * N_LAT * N_LON)
    row0 = jnp.where(flat == chosen, CTH - 2, row0)
    col0 = jnp.where(flat == chosen, CPH - 2, col0)
    anchor = row0 * CPH + col0
    offsets = jnp.array([0, 1, CPH, CPH + 1], dtype=jnp.int32)
    cells = anchor[..., None] + offsets
    return cells.reshape(N_PANEL, N_LAT, N_LON, N_LAT * N_LON * CAP).astype(jnp.int32)


def draw_partner(key, part):
    key = jax.random.fold_in(key, 5)
    keys = jax.random.split(key, 3)
    shape = (N_PANEL, N_LAT, N_LON)
    lat_c = jax.random.randint(keys[0], shape, 0, N_LAT - 1)
    lon_c = jax.random.randint(keys[1], shape, 0, N_LON - 1)
    flat = jnp.arange(N_PANEL * N_LAT * N_LON, dtype=jnp.int32).reshape(shape)
    chosen = jax.random.randint(keys[2], (), 0, N_PANEL * N_LAT * N_LON)
    lat_c = jnp.where(flat == chosen, N_LAT - 2, lat_c)
    lon_c = jnp.where(flat == chosen, N_LON - 2, lon_c)
    base = lat_c * N_LON + lon_c
    return jnp.stack([base, base + 1, base + N_LON, base + N_LON + 1], axis=-1).astype(jnp.int32)


def set_ends(entries, own_key, least, high):
    dims = entries.shape
    place = [jax.random.randint(jax.random.fold_in(own_key, axis), (), 0, dims[axis]) for axis in range(len(dims))]
    entries = entries.at[tuple(place)].set(least)
    longest = dims.index(max(dims))
    place[longest] = (place[longest] + 1) % dims[longest]
    return entries.at[tuple(place)].set(high)


def level_of(key, extent, shards, least, largest):
    loudness, own = 1.0, jax.random.fold_in(key, 6)
    for axis_at, blocks in shards:
        heights = jnp.exp(jax.random.uniform(jax.random.fold_in(own, axis_at), (blocks,), jnp.float32, least / len(shards), largest / len(shards)))
        loudness = loudness * jnp.repeat(heights, extent[axis_at] // blocks).reshape([-1 if axis == axis_at else 1 for axis in range(len(extent))])
    return loudness


def noise(own_key, extent, spread, reach, pieces=(), held_as=jnp.bfloat16):
    result = spread * jax.random.normal(own_key, extent, jnp.float32)
    if pieces:
        result = result * level_of(own_key, extent, pieces, -0.22, 0.18)
    return jnp.clip(result, -reach, reach).astype(held_as)


def setup_inputs(seed: int = 0) -> dict:
    key_list = jax.random.split(jax.random.key(seed), 8)
    viscosity = draw_viscosity(jax.random.fold_in(key_list[7], 71), 0)
    forcing = noise(key_list[1], (4, N_PANEL, NTH, NPH, NR), 1.0, 6.0, ((1, 2), (2, 8), (3, 32)), jnp.float32)
    send_cell = draw_send_cell(jax.random.fold_in(key_list[7], 71), 0)
    partner = draw_partner(jax.random.fold_in(key_list[7], 71), 0)
    ghost_src = set_ends(jax.random.randint(key_list[4], (N_PANEL, N_LAT, N_LON, GH), 0, 4), jax.random.fold_in(key_list[4], 1), 0, 3).astype(jnp.int32)
    ghost_weight = jnp.clip(0.05 + 0.95 * jax.random.uniform(key_list[5], (N_PANEL, N_LAT, N_LON, GH, CAP), jnp.float32) ** level_of(key_list[5], (N_PANEL, N_LAT, N_LON, GH, CAP), ((0, 2), (1, 8), (2, 32)), -0.2, 0.2), 0.05, 1.0)
    ghost_angle = jnp.clip(jax.random.uniform(key_list[6], (N_PANEL, N_LAT, N_LON, GH), jnp.float32, -3.140625, 3.140625), -3.140625, 3.140625)
    return {"viscosity": viscosity, "forcing": forcing, "send_cell": send_cell, "partner": partner, "ghost_src": ghost_src, "ghost_weight": ghost_weight, "ghost_angle": ghost_angle}


def shifted(a, axis, off):
    lead = a.ndim - 3
    size = a.shape[lead + axis]
    index = [slice(1, -1)] * 3
    index[axis] = slice(1 + off, size - 1 + off)
    return a[tuple([slice(None)] * lead + index)]

def sweep(padded, padded_visc, forcing, state):
    root = jnp.sqrt(padded_visc)
    six = jnp.sqrt(6.0)
    velocity = padded[:3] / (six * root)
    pressure = padded[3] * root
    centre_visc = shifted(padded_visc, 0, 0)
    centre_vel = shifted(velocity, 0, 0)
    lap = jnp.zeros_like(centre_vel)
    dsum = jnp.zeros_like(centre_visc)
    grads = []
    div = jnp.zeros_like(centre_visc)
    for axis in range(3):
        for off in (-1, 1):
            other = shifted(padded_visc, axis, off)
            face = 2.0 * centre_visc * other / (centre_visc + other)
            dsum = dsum + face
            lap = lap + face * (centre_vel - shifted(velocity, axis, off))
        grads.append(0.5 * (shifted(pressure, axis, 1) - shifted(pressure, axis, -1)))
        div = div + 0.5 * (shifted(velocity[axis], axis, 1) - shifted(velocity[axis], axis, -1))
    image_vel = (lap + jnp.stack(grads)) / (six * jnp.sqrt(centre_visc))
    image_pre = (-div - shifted(pressure, 0, 0) / centre_visc) * jnp.sqrt(centre_visc)
    new_vel = state[:3] + 0.5 * (forcing[:3] - image_vel) * 6.0 * centre_visc / dsum
    new_pre = state[3] - 0.5 * (forcing[3] - image_pre)
    return jnp.concatenate([new_vel, new_pre[None]], axis=0)

def reference(viscosity, forcing, send_cell, partner, ghost_src, ghost_weight, ghost_angle):
    nl = N_LAT
    no = N_LON
    padded_visc = jnp.pad(viscosity, ((0, 0), (1, 1), (1, 1), (1, 1)), mode='edge')
    norm_weight = ghost_weight / lax.optimization_barrier(jnp.sum(ghost_weight, axis=-1, keepdims=True))
    chosen = jnp.take_along_axis(partner, ghost_src, axis=3)
    donors = chosen[..., None] * CAP + jnp.arange(CAP, dtype=jnp.int32)
    donors = donors.astype(jnp.int32).reshape(2, nl, no, GH * CAP)
    cosine = jnp.cos(ghost_angle)[None, ..., None]
    sine = jnp.sin(ghost_angle)[None, ..., None]
    state = jnp.zeros_like(forcing)
    for step in range(ITERS):
        blocks = state.reshape(4, 2, nl, CTH, no, CPH, NR).transpose(0, 1, 2, 4, 3, 5, 6)
        blocks = blocks.reshape(4, 2, nl, no, CTH * CPH, NR)
        packed = jnp.take_along_axis(blocks, send_cell[None, ..., None], axis=4)
        packed = packed.reshape(4, 2, nl * no, nl * no, CAP, NR)
        received = jnp.flip(packed, 1).transpose(0, 1, 3, 2, 4, 5).reshape(4, 2, nl, no, SENDS, NR)
        picked = jnp.take_along_axis(received, donors[None, ..., None], axis=4)
        picked = picked.reshape(4, 2, nl, no, GH, CAP, NR)
        ghost = lax.optimization_barrier(jnp.sum(picked * norm_weight[None, ..., None], axis=5))
        rot_u = cosine[0] * ghost[0] - sine[0] * ghost[1]
        rot_v = sine[0] * ghost[0] + cosine[0] * ghost[1]
        ghost = jnp.concatenate([rot_u[None], rot_v[None], ghost[2:]], axis=0)
        south = ghost[:, :, 0, :, 0:CPH].reshape(4, 2, NPH, NR)
        north = ghost[:, :, nl - 1, :, CPH:2 * CPH].reshape(4, 2, NPH, NR)
        west = ghost[:, :, :, 0, 2 * CPH:2 * CPH + CTH].reshape(4, 2, NTH, NR)
        east = ghost[:, :, :, no - 1, 2 * CPH + CTH:].reshape(4, 2, NTH, NR)
        padded = jnp.pad(state, ((0, 0), (0, 0), (1, 1), (1, 1), (1, 1)))
        padded = padded.at[:, :, 0, 1:-1, 1:-1].set(south)
        padded = padded.at[:, :, -1, 1:-1, 1:-1].set(north)
        padded = padded.at[:, :, 1:-1, 0, 1:-1].set(west)
        padded = padded.at[:, :, 1:-1, -1, 1:-1].set(east)
        state = sweep(padded, padded_visc, forcing, state)
    return state
```

```python
import math

import jax
import jax.numpy as jnp
from jax import lax
from jax.experimental import pallas as pl
from jax.experimental.pallas import tpu as pltpu
from jax.sharding import PartitionSpec as P

MESH = pl.DeviceIdType.MESH
LAT, LON = 8, 32
ROWS, COLS, DEPTH = 8, 16, 128
CELLS = ROWS * COLS
GHOSTS = 48
PIECE = 4 * DEPTH // LON
C0 = 8
F32, I32 = jnp.float32, jnp.int32


def copy_to(src, dst, send, recv, device):
    pltpu.make_async_remote_copy(
        src_ref=src,
        dst_ref=dst,
        send_sem=send,
        recv_sem=recv,
        device_id=device,
        device_id_type=MESH,
    ).start()


def take_bytes(ref, sem):
    pltpu.make_async_copy(ref, ref, sem).wait()


def iota(shape, dim):
    return lax.broadcasted_iota(I32, shape, dim)


def kernel(
    visc, rhs, cells, partner, src, weight, angle, out,
    pv, hv_row, hv_col, hv_srow, hv_scol,
    xs, face, coef, force, root,
    h_srow, h_scol, h_row, h_col,
    meta, metas, bases, other_bases,
    tb, r1, xb, xbi, xr, zb, dd, ghost,
    sem_hv, sem_m, sem_b, sem_h, sem_1, sem_2, sem_3,
):
    p = lax.axis_index("panel")
    i = lax.axis_index("lat")
    j = lax.axis_index("lon")
    q = 1 - p
    lat_edge = jnp.logical_or(i == 0, i == LAT - 1)
    lon_edge = jnp.logical_or(j == 0, j == LON - 1)
    is_edge = jnp.logical_or(lat_edge, lon_edge)

    def at_lon(jj):
        return {"panel": p, "lat": i, "lon": jj}

    def at_lat(ii):
        return {"panel": p, "lat": ii, "lon": j}

    def across(ii):
        return {"panel": q, "lat": ii, "lon": j}

    south, north = lax.rem(i + LAT - 1, LAT), lax.rem(i + 1, LAT)
    west, east = lax.rem(j + LON - 1, LON), lax.rem(j + 1, LON)

    barrier = pltpu.get_barrier_semaphore()

    def greet(o, c):
        pl.semaphore_signal(barrier, 1, device_id=at_lon(lax.rem(j + o, LON)), device_id_type=MESH)
        return c

    def greet_across(o, c):
        pl.semaphore_signal(barrier, 1, device_id=across(o), device_id_type=MESH)
        return c

    lax.fori_loop(0, LAT, greet_across, 0)
    pl.semaphore_signal(barrier, 1, device_id=at_lat(south), device_id_type=MESH)
    pl.semaphore_signal(barrier, 1, device_id=at_lat(north), device_id_type=MESH)
    lax.fori_loop(1, LON, greet, 0)

    sub8 = iota((8, 128), 0)
    lane8 = iota((8, 128), 1)
    lane16 = iota((16, 128), 1)
    cell_of = cells[...]
    mine = jnp.where(lane8 % 4 == 0, cell_of, 0)
    meta[...] = jnp.where(lane8 == 4 * j + 1, partner[0], mine)
    hv_srow[0] = visc[0]
    hv_srow[1] = visc[ROWS - 1]
    for r in range(ROWS):
        hv_scol[0, r : r + 1, :] = visc[r, 0:1, :]
        hv_scol[1, r : r + 1, :] = visc[r, COLS - 1 : COLS, :]
    pv[1 : ROWS + 1, C0 : C0 + COLS, :] = visc[...]
    metas[pl.ds(j, 1)] = meta[...][None]

    pl.semaphore_wait(barrier, LAT + 2 + LON - 1)

    copy_to(hv_srow.at[0], hv_row.at[1], sem_hv.at[0], sem_hv.at[1], at_lat(south))
    copy_to(hv_srow.at[1], hv_row.at[0], sem_hv.at[0], sem_hv.at[1], at_lat(north))
    copy_to(hv_scol.at[0], hv_col.at[1], sem_hv.at[3], sem_hv.at[2], at_lon(west))
    copy_to(hv_scol.at[1], hv_col.at[0], sem_hv.at[3], sem_hv.at[2], at_lon(east))

    def send_meta(o, c):
        copy_to(meta, metas.at[j], sem_m.at[0], sem_m.at[1], at_lon(lax.rem(j + o, LON)))
        return c

    lax.fori_loop(1, LON, send_meta, 0)

    take_bytes(hv_row, sem_hv.at[1])
    take_bytes(hv_col, sem_hv.at[2])
    pv[0, C0 : C0 + COLS, :] = jnp.where(i == 0, visc[0], hv_row[0])
    pv[ROWS + 1, C0 : C0 + COLS, :] = jnp.where(i == LAT - 1, visc[ROWS - 1], hv_row[1])
    first = jnp.where(j == 0, hv_scol[0], hv_col[0])
    last = jnp.where(j == LON - 1, hv_scol[1], hv_col[1])
    for r in range(ROWS):
        pv[1 + r, C0 - 1 : C0, :] = first[r : r + 1, :]
        pv[1 + r, C0 + COLS : C0 + COLS + 1, :] = last[r : r + 1, :]

    def ahead(v):
        return pltpu.roll(v, DEPTH - 1, 1)

    def behind(v):
        return pltpu.roll(v, 1, 1)

    top, bottom = lane16 == DEPTH - 1, lane16 == 0

    def prepare(r, c):
        e = pv[1 + r, C0 : C0 + COLS, :]
        near = (
            pv[r, C0 : C0 + COLS, :],
            pv[2 + r, C0 : C0 + COLS, :],
            pv[1 + r, C0 - 1 : C0 - 1 + COLS, :],
            pv[1 + r, C0 + 1 : C0 + 1 + COLS, :],
            jnp.where(bottom, e, behind(e)),
            jnp.where(top, e, ahead(e)),
        )
        dsum = jnp.zeros_like(e)
        for k, o in enumerate(near):
            f = 2.0 * e * o / (e + o)
            face[k, r] = f
            dsum = dsum + f
        half = 0.5 / dsum
        coef[r] = half
        se = jnp.sqrt(e)
        six = math.sqrt(6.0) * se
        root[0, r] = se
        root[1, r] = six
        root[2, r] = 1.0 / se
        for a in range(3):
            w = rhs[a, r] * six
            force[a, r] = w
            x = half * w
            xs[a, 1 + r, C0 : C0 + COLS, :] = x
            tb[0, a, r * COLS : (r + 1) * COLS, :] = x * six
        force[3, r] = -0.5 * (rhs[3, r] * se)
        xs[3, 1 + r, C0 : C0 + COLS, :] = -0.5 * (rhs[3, r] * se)
        tb[0, 3, r * COLS : (r + 1) * COLS, :] = -0.5 * rhs[3, r]
        return c

    for r in range(ROWS):
        prepare(r, 0)

    def sweep(out_at):
        for r in range(ROWS):
            def get(a, dr, dc):
                return xs[a, 1 + r + dr, C0 + dc : C0 + dc + COLS, :]

            e = pv[1 + r, C0 : C0 + COLS, :]
            half = coef[r]
            around = []
            for a in range(4):
                v = get(a, 0, 0)
                around.append(
                    (
                        get(a, -1, 0),
                        get(a, 1, 0),
                        get(a, 0, -1),
                        get(a, 0, 1),
                        jnp.where(bottom, 0.0, behind(v)),
                        jnp.where(top, 0.0, ahead(v)),
                        v,
                    )
                )
            pr = around[3]
            div = jnp.zeros_like(e)
            for a in range(3):
                total = force[a, r] - 0.5 * (pr[2 * a + 1] - pr[2 * a])
                for k in range(6):
                    total = total + face[k, r] * around[a][k]
                x = 0.5 * around[a][6] + half * total
                out_at(a, r, x)
                div = div + (around[a][2 * a + 1] - around[a][2 * a])
            out_at(3, r, 0.5 * pr[6] + force[3, r] - 0.25 * (e * div))

    def start_phase_1(n):
        for a in range(4):
            t = tb[n, a].T
            tb[n, a] = t

        def send(o, c):
            jj = lax.rem(j + o, LON)
            a, b = jj // 8, lax.rem(jj, 8)
            copy_to(
                tb.at[n, a, pl.ds(b * PIECE, PIECE)],
                r1.at[n, j],
                sem_1.at[n, 0],
                sem_1.at[n, 1],
                at_lon(jj),
            )
            return c

        lax.fori_loop(1, LON, send, 0)
        r1[n, pl.ds(j, 1)] = tb[n, pl.ds(j // 8, 1), pl.ds(lax.rem(j, 8) * PIECE, PIECE)]

    def start_halo(n):
        for a in range(4):
            h_srow[n, 0, a] = xs[a, 1, C0 : C0 + COLS, :]
            h_srow[n, 1, a] = xs[a, ROWS, C0 : C0 + COLS, :]
            for r in range(ROWS):
                h_scol[n, 0, a, r : r + 1, :] = xs[a, 1 + r, C0 : C0 + 1, :]
                h_scol[n, 1, a, r : r + 1, :] = xs[a, 1 + r, C0 + COLS - 1 : C0 + COLS, :]
        copy_to(h_srow.at[n, 0], h_row.at[n, 1], sem_h.at[n, 0], sem_h.at[n, 1], at_lat(south))
        copy_to(h_srow.at[n, 1], h_row.at[n, 0], sem_h.at[n, 0], sem_h.at[n, 1], at_lat(north))
        copy_to(h_scol.at[n, 0], h_col.at[n, 1], sem_h.at[n, 3], sem_h.at[n, 2], at_lon(west))
        copy_to(h_scol.at[n, 1], h_col.at[n, 0], sem_h.at[n, 3], sem_h.at[n, 2], at_lon(east))

    start_phase_1(0)
    start_halo(0)

    take_bytes(metas.at[pl.ds(0, LON - 1)], sem_m.at[1])
    total = jnp.zeros((8, 128), I32)
    for c in range(LON):
        total = total + metas[c]
    own = jnp.where(lane8 % 4 == 1, total, 0)
    own = pltpu.roll(own, 127, 1) + own + pltpu.roll(own, 1, 1) + pltpu.roll(own, 2, 1)
    bases[...] = own

    def send_bases(o, c):
        copy_to(bases, other_bases.at[i], sem_b.at[0], sem_b.at[1], across(o))
        return c

    lax.fori_loop(0, LAT, send_bases, 0)

    def column(row):
        return jnp.broadcast_to(row, (128, 128)).T[0:GHOSTS]

    source = column(src[...])
    cosine = column(jnp.cos(angle[...]))
    sine = column(jnp.sin(angle[...]))
    wk = weight[...]
    wk = wk / jnp.sum(wk, axis=1, keepdims=True)
    lane48 = iota((GHOSTS, 128), 1)
    mix = jnp.zeros((GHOSTS, 128), F32)
    for k in range(4):
        mix = mix + jnp.where(lane48 % 4 == k, wk[:, k : k + 1], 0.0)
    which = lane48 // 8 + 2 * (lane48 // 4 % 2)
    mix = jnp.where(jnp.logical_and(which == source, lane48 < 16), mix, 0.0)[:, 0:16]

    take_bytes(other_bases, sem_b.at[1])
    base = jnp.zeros((8, 128), I32)
    for r in range(LAT):
        base = base + jnp.where(sub8 == r, other_bases[r], 0)
    col = base & (LON - 1)
    offset = (lane8 & 1) + COLS * ((lane8 // 2) & 1)
    pick = []
    for t in range(2):
        a = jnp.zeros((8, 128), I32)
        for c in range(LON):
            a = a + jnp.where(col + t == c, metas[c], 0)
        a = jnp.where(lane8 % 4 == 0, a, 0)
        pick.append(a + pltpu.roll(a, 1, 1) + pltpu.roll(a, 2, 1) + pltpu.roll(a, 3, 1) + offset)

    def inner(v):
        w = jnp.zeros((8, 128), I32)
        for r in range(1, LAT - 1):
            here = jnp.logical_and(lane8 >= 8 * r - 4, lane8 < 8 * r + 4)
            row = jnp.broadcast_to(v[r : r + 1, :], (8, 128))
            w = w + jnp.where(here, pltpu.roll(row, 8 * r, 1), 0)
        return w[0:1]

    def wide(row):
        return jnp.broadcast_to(row, (PIECE, 128))

    groups = []
    for g in range(3):
        def of(v):
            return wide(inner(v) if g == 2 else v[7 * g : 7 * g + 1, :])
        groups.append((of(col), of(pick[0]), of(pick[1])))

    own_row = own >> 5
    packed_row = jnp.where(lane8 < 64, pltpu.roll(own_row, 8 * i, 1), pltpu.roll(own_row, 8 * i + 64, 1))
    rows_full = jnp.broadcast_to(own_row[0:1], (PIECE, 128))
    rows_packed = jnp.broadcast_to(packed_row[0:1], (PIECE, 128))

    def ghost_columns(n):
        take_bytes(r1.at[n, pl.ds(0, LON - 1)], sem_1.at[n, 1])
        picked = []
        for g in range(3):
            at_col, first, second = groups[g]
            for t in range(2):
                index = second if t else first
                acc = jnp.zeros((PIECE, 128), F32)
                for c in range(LON):
                    v = jnp.take_along_axis(r1[n, c], index, axis=1, mode="promise_in_bounds")
                    acc = jnp.where(at_col == c - t, v, acc)
                picked.append(acc)
        for g in range(2):
            for t in range(2):
                xb[n, g, t] = picked[2 * g + t]
        xbi[n] = jnp.where(lane16 < 64, picked[4], pltpu.roll(picked[5], 64, 1))

        copy_to(xb.at[n, 0], xr.at[n, i], sem_2.at[n, 0], sem_2.at[n, 1], across(0))
        copy_to(xb.at[n, 1], xr.at[n, i], sem_2.at[n, 0], sem_2.at[n, 1], across(LAT - 1))

        def send_inner(o, c):
            copy_to(xbi.at[n], xr.at[n, i, 0], sem_2.at[n, 2], sem_2.at[n, 1], across(o))
            return c

        lax.fori_loop(1, LAT - 1, send_inner, 0)

        def turn(y):
            z = jnp.concatenate([y[0][0], y[1][0], y[0][1], y[1][1]], axis=0)
            z = jnp.concatenate([z, z], axis=0).T
            for jj in range(LON):
                zb[n, jj] = z[4 * jj : 4 * jj + 4, :]

        @pl.when(lat_edge)
        def _():
            take_bytes(xr.at[n], sem_2.at[n, 1])
            y = []
            for s in range(2):
                pair = []
                for t in range(2):
                    acc = jnp.zeros((PIECE, 128), F32)
                    for r in range(LAT):
                        acc = jnp.where(rows_full + s == r, xr[n, r, t], acc)
                    pair.append(acc)
                y.append(pair)
            turn(y)

            def send(o, c):
                jj = lax.rem(j + o, LON)
                copy_to(zb.at[n, jj], dd.at[n, j], sem_3.at[n, 0], sem_3.at[n, 1], at_lon(jj))
                return c

            lax.fori_loop(1, LON, send, 0)

        @pl.when(jnp.logical_not(lat_edge))
        def _():
            take_bytes(xr.at[n, :, 0], sem_2.at[n, 1])
            y = []
            for s in range(2):
                acc = jnp.zeros((PIECE, 128), F32)
                for r in range(LAT):
                    acc = jnp.where(rows_packed + s == r, xr[n, r, 0], acc)
                y.append([pltpu.roll(acc, lax.rem(128 - 8 * i, 128), 1), pltpu.roll(acc, 64 - 8 * i, 1)])
            turn(y)

            @pl.when(j != 0)
            def _():
                copy_to(zb.at[n, 0], dd.at[n, j], sem_3.at[n, 0], sem_3.at[n, 1], at_lon(0))

            @pl.when(j != LON - 1)
            def _():
                copy_to(zb.at[n, LON - 1], dd.at[n, j], sem_3.at[n, 0], sem_3.at[n, 1], at_lon(LON - 1))

        @pl.when(is_edge)
        def _():
            dd[n, pl.ds(j, 1)] = zb[n, pl.ds(j, 1)]
            take_bytes(dd.at[n, pl.ds(0, LON - 1)], sem_3.at[n, 1])
            lane4 = iota((4, 128), 1)
            g = []
            for a in range(4):
                parts = []
                for k in range(4):
                    v = jnp.zeros((4, 128), F32)
                    for b in range(8):
                        turned = pltpu.roll(dd[n, 8 * a + b], (PIECE * (b - k)) % 128, 1)
                        v = jnp.where(lane4 // PIECE == b, turned, v)
                    parts.append(v)
                cells_at = jnp.concatenate(parts, axis=0)
                g.append(
                    lax.dot_general(
                        mix, cells_at, (((1,), (0,)), ((), ())),
                        precision=lax.Precision.HIGHEST, preferred_element_type=F32,
                    )
                )
            ghost[0] = cosine * g[0] - sine * g[1]
            ghost[1] = sine * g[0] + cosine * g[1]
            ghost[2] = g[2]
            ghost[3] = g[3]

    def fill_halo(n):
        take_bytes(h_row.at[n], sem_h.at[n, 1])
        take_bytes(h_col.at[n], sem_h.at[n, 2])
        for side, edge, r_in, r_out in ((0, 0, 0, 0), (1, LAT - 1, ROWS - 1, ROWS + 1)):
            @pl.when(i != edge)
            def _():
                for a in range(4):
                    xs[a, r_out, C0 : C0 + COLS, :] = h_row[n, side, a]

            @pl.when(i == edge)
            def _():
                for a in range(4):
                    v = ghost[a, side * COLS : (side + 1) * COLS, :]
                    v = v * root[0, r_in] if a == 3 else v / root[1, r_in]
                    xs[a, r_out, C0 : C0 + COLS, :] = v

        for side, edge, c_in, c_out in ((0, 0, 0, C0 - 1), (1, LON - 1, COLS - 1, C0 + COLS)):
            @pl.when(j != edge)
            def _():
                for a in range(4):
                    for r in range(ROWS):
                        xs[a, 1 + r, c_out : c_out + 1, :] = h_col[n, side, a, r : r + 1, :]

            @pl.when(j == edge)
            def _():
                at = 2 * COLS + side * ROWS
                for a in range(4):
                    for r in range(ROWS):
                        v = ghost[a, at + r : at + r + 1, :]
                        if a == 3:
                            v = v * root[0, r, c_in : c_in + 1, :]
                        else:
                            v = v / root[1, r, c_in : c_in + 1, :]
                        xs[a, 1 + r, c_out : c_out + 1, :] = v

    ghost_columns(0)
    fill_halo(0)
    fresh = {}

    def keep(a, r, v):
        fresh[a, r] = v

    def to_state(a, r, v):
        return v * (root[2, r] if a == 3 else root[1, r])

    def second(a, r, v):
        tb[1, a, r * COLS : (r + 1) * COLS, :] = v

    sweep(second)
    for r in range(ROWS):
        for a in range(4):
            v = tb[1, a, r * COLS : (r + 1) * COLS, :]
            xs[a, 1 + r, C0 : C0 + COLS, :] = v
            tb[1, a, r * COLS : (r + 1) * COLS, :] = to_state(a, r, v)
    start_phase_1(1)
    start_halo(1)
    ghost_columns(1)
    fill_halo(1)

    def third(a, r, v):
        out[a, r] = to_state(a, r, v)

    sweep(third)

    take_bytes(hv_row, sem_hv.at[0])
    take_bytes(hv_col, sem_hv.at[3])
    take_bytes(metas.at[pl.ds(0, LON - 1)], sem_m.at[0])
    take_bytes(other_bases, sem_b.at[0])
    for n in range(2):
        take_bytes(h_row.at[n], sem_h.at[n, 0])
        take_bytes(h_col.at[n], sem_h.at[n, 3])
        take_bytes(r1.at[n, pl.ds(0, LON - 1)], sem_1.at[n, 0])
        take_bytes(xb.at[n], sem_2.at[n, 0])
        take_bytes(r1.at[n, pl.ds(0, LAT - 2)], sem_2.at[n, 2])

        @pl.when(lat_edge)
        def _():
            take_bytes(dd.at[n, pl.ds(0, LON - 1)], sem_3.at[n, 0])

        @pl.when(jnp.logical_not(lat_edge))
        def _():
            @pl.when(lon_edge)
            def _():
                take_bytes(dd.at[n, 0], sem_3.at[n, 0])

            @pl.when(jnp.logical_not(lon_edge))
            def _():
                take_bytes(dd.at[n, pl.ds(0, 2)], sem_3.at[n, 0])


def body(viscosity, forcing, send_cell, partner, ghost_src, ghost_weight, ghost_angle):
    vmem = pl.BlockSpec(memory_space=pltpu.VMEM)
    smem = pl.BlockSpec(memory_space=pltpu.SMEM)
    dma = pltpu.SemaphoreType.DMA
    pad = ((0, 0), (0, 128 - GHOSTS))
    scratch = [
        pltpu.VMEM((ROWS + 2, C0 + COLS + 8, DEPTH), F32),
        pltpu.VMEM((2, COLS, DEPTH), F32),
        pltpu.VMEM((2, ROWS, DEPTH), F32),
        pltpu.VMEM((2, COLS, DEPTH), F32),
        pltpu.VMEM((2, ROWS, DEPTH), F32),
        pltpu.VMEM((4, ROWS + 2, C0 + COLS + 8, DEPTH), F32),
        pltpu.VMEM((6, ROWS, COLS, DEPTH), F32),
        pltpu.VMEM((ROWS, COLS, DEPTH), F32),
        pltpu.VMEM((4, ROWS, COLS, DEPTH), F32),
        pltpu.VMEM((3, ROWS, COLS, DEPTH), F32),
        pltpu.VMEM((2, 2, 4, COLS, DEPTH), F32),
        pltpu.VMEM((2, 2, 4, ROWS, DEPTH), F32),
        pltpu.VMEM((2, 2, 4, COLS, DEPTH), F32),
        pltpu.VMEM((2, 2, 4, ROWS, DEPTH), F32),
        pltpu.VMEM((8, 128), I32),
        pltpu.VMEM((LON, 8, 128), I32),
        pltpu.VMEM((8, 128), I32),
        pltpu.VMEM((LAT, 8, 128), I32),
        pltpu.VMEM((2, 4, CELLS, DEPTH), F32),
        pltpu.VMEM((2, LON, PIECE, CELLS), F32),
        pltpu.VMEM((2, 2, 2, PIECE, 128), F32),
        pltpu.VMEM((2, PIECE, 128), F32),
        pltpu.VMEM((2, LAT, 2, PIECE, 128), F32),
        pltpu.VMEM((2, LON, 4, 128), F32),
        pltpu.VMEM((2, LON, 4, 128), F32),
        pltpu.VMEM((4, GHOSTS, DEPTH), F32),
        dma((4,)), dma((2,)), dma((2,)), dma((2, 4)), dma((2, 2)), dma((2, 3)), dma((2, 2)),
    ]
    state = pl.pallas_call(
        kernel,
        out_shape=jax.ShapeDtypeStruct((4, ROWS, COLS, DEPTH), F32),
        in_specs=[vmem, vmem, vmem, smem, vmem, vmem, vmem],
        out_specs=vmem,
        scratch_shapes=scratch,
        compiler_params=pltpu.CompilerParams(
            collective_id=0, has_side_effects=True, vmem_limit_bytes=32 << 20
        ),
    )(
        viscosity.reshape(ROWS, COLS, DEPTH),
        forcing.reshape(4, ROWS, COLS, DEPTH),
        send_cell.reshape(LAT, 4 * LON),
        partner.reshape(4),
        jnp.pad(ghost_src.reshape(1, GHOSTS), pad),
        ghost_weight.reshape(GHOSTS, 4),
        jnp.pad(ghost_angle.reshape(1, GHOSTS), pad),
    )
    return state[:, None]


def solution(mesh):
    placed = (
        P("panel", "lat", "lon", None),
        P(None, "panel", "lat", "lon", None),
        P("panel", "lat", "lon", None),
        P("panel", "lat", "lon", None),
        P("panel", "lat", "lon", None),
        P("panel", "lat", "lon", None, None),
        P("panel", "lat", "lon", None),
    )
    return jax.shard_map(
        body,
        mesh=mesh,
        in_specs=placed,
        out_specs=P(None, "panel", "lat", "lon", None),
        check_vma=False,
    )
```

```python
import math

import jax
import jax.numpy as jnp
from jax import lax
from jax.experimental import pallas as pl
from jax.experimental.pallas import tpu as pltpu
from jax.sharding import PartitionSpec as P

MESH = pl.DeviceIdType.MESH
LAT, LON = 8, 32
ROWS, COLS, DEPTH = 8, 16, 128
CELLS = ROWS * COLS
GHOSTS = 48
PIECE = 4 * DEPTH // LON
C0 = 8
F32, I32 = jnp.float32, jnp.int32
SIX = math.sqrt(6.0)
THIRD = 0.25 / SIX


def copy_to(src, dst, send, recv, device):
    pltpu.make_async_remote_copy(
        src_ref=src,
        dst_ref=dst,
        send_sem=send,
        recv_sem=recv,
        device_id=device,
        device_id_type=MESH,
    ).start()


def take_bytes(ref, sem):
    pltpu.make_async_copy(ref, ref, sem).wait()


def iota(shape, dim):
    return lax.broadcasted_iota(I32, shape, dim)


def kernel(
    visc_in, rhs_in, cells_in, partner_in, src_in, angle_in, weight_in, out,
    visc, rhs, cells, partner, src, angle, weight,
    pv, hv_row, hv_col, hv_srow, hv_scol,
    xs, face, coef, force, root,
    h_srow, h_scol, h_row, h_col,
    meta, metas, bases, other_bases, info, infos, square,
    nat, tb, r1, rc, xb, xbi, xr, ys, zb, dd, turned, ghost, wv, ww,
    sem_in, sem_hv, sem_m, sem_i, sem_b, sem_h, sem_1, sem_c, sem_2, sem_3,
):
    p = lax.axis_index("panel")
    i = lax.axis_index("lat")
    j = lax.axis_index("lon")
    q = 1 - p
    lat_edge = jnp.logical_or(i == 0, i == LAT - 1)
    lon_edge = jnp.logical_or(j == 0, j == LON - 1)
    is_edge = jnp.logical_or(lat_edge, lon_edge)

    def at_lon(jj):
        return {"panel": p, "lat": i, "lon": jj}

    def at_lat(ii):
        return {"panel": p, "lat": ii, "lon": j}

    def across(ii):
        return {"panel": q, "lat": ii, "lon": j}

    south, north = lax.rem(i + LAT - 1, LAT), lax.rem(i + 1, LAT)
    west, east = lax.rem(j + LON - 1, LON), lax.rem(j + 1, LON)

    def to_row(n, send):
        def step(o, c):
            send(lax.rem(j + o, LON))
            return c

        lax.fori_loop(1, LON, step, 0)

    barrier = pltpu.get_barrier_semaphore()

    def greet(device):
        pl.semaphore_signal(barrier, 1, device_id=device, device_id_type=MESH)

    def greet_across(o, c):
        greet(across(o))
        return c

    lax.fori_loop(0, LAT, greet_across, 0)
    greet(at_lat(south))
    greet(at_lat(north))
    to_row(0, lambda jj: greet(at_lon(jj)))

    moves = [
        pltpu.make_async_copy(a, b, sem_in.at[n])
        for n, (a, b) in enumerate(
            (
                (visc_in, visc), (cells_in, cells), (partner_in, partner), (weight_in, weight),
                (src_in, src), (angle_in, angle), (rhs_in, rhs),
            )
        )
    ]
    for move in moves:
        move.start()
    for move in moves:
        move.wait()
    sub8 = iota((8, 128), 0)
    lane8 = iota((8, 128), 1)
    lane16 = iota((16, 128), 1)
    low8 = sub8 < 4
    meta[...] = jnp.where(
        lane8 == 4 * j + 1, partner[...], jnp.where(lane8 % 4 == 0, cells[...], 0)
    )
    metas[pl.ds(j, 1)] = meta[...][None]
    hv_srow[0] = visc[0]
    hv_srow[1] = visc[ROWS - 1]
    for r in range(ROWS):
        hv_scol[0, r : r + 1, :] = visc[r, 0:1, :]
        hv_scol[1, r : r + 1, :] = visc[r, COLS - 1 : COLS, :]
    pv[1 : ROWS + 1, C0 : C0 + COLS, :] = visc[...]

    def column(row):
        return jnp.broadcast_to(row, (128, 128)).T[0:GHOSTS]

    cos_row, sin_row = jnp.cos(angle[...]), jnp.sin(angle[...])
    source = column(src[...])
    cosine = column(cos_row)
    sine = column(sin_row)
    wk = weight[...]
    wk = wk / jnp.sum(wk, axis=1, keepdims=True)
    lane48 = iota((GHOSTS, 128), 1)
    spread = jnp.zeros((GHOSTS, 128), F32)
    for k in range(4):
        spread = spread + jnp.where(lane48 == k, wk[:, k : k + 1], 0.0)
    square[...] = jnp.zeros((128, 128), F32)
    square[0:GHOSTS, :] = spread
    info[0:4, :] = square[...].T[0:4]
    info[4:5, :] = cos_row
    info[5:6, :] = sin_row
    info[6:7, :] = src[...].astype(F32)
    info[7:8, :] = cos_row
    infos[pl.ds(j, 1)] = info[...][None]
    mix = jnp.zeros((GHOSTS, 128), F32)
    for k in range(4):
        mix = mix + jnp.where(lane48 // 4 == k, wk[:, k : k + 1], 0.0)
    which = lane48 // 2 % 2 + 2 * (lane48 % 2)
    mix = jnp.where(which == source, mix, 0.0)[:, 0:16]

    pl.semaphore_wait(barrier, LAT + 2 + LON - 1)

    copy_to(hv_srow.at[0], hv_row.at[1], sem_hv.at[0], sem_hv.at[1], at_lat(south))
    copy_to(hv_srow.at[1], hv_row.at[0], sem_hv.at[0], sem_hv.at[1], at_lat(north))
    copy_to(hv_scol.at[0], hv_col.at[1], sem_hv.at[3], sem_hv.at[2], at_lon(west))
    copy_to(hv_scol.at[1], hv_col.at[0], sem_hv.at[3], sem_hv.at[2], at_lon(east))
    to_row(0, lambda jj: copy_to(meta, metas.at[j], sem_m.at[0], sem_m.at[1], at_lon(jj)))

    take_bytes(hv_row, sem_hv.at[1])
    take_bytes(hv_col, sem_hv.at[2])
    pv[0, C0 : C0 + COLS, :] = jnp.where(i == 0, visc[0], hv_row[0])
    pv[ROWS + 1, C0 : C0 + COLS, :] = jnp.where(i == LAT - 1, visc[ROWS - 1], hv_row[1])
    first = jnp.where(j == 0, hv_scol[0], hv_col[0])
    last = jnp.where(j == LON - 1, hv_scol[1], hv_col[1])
    for r in range(ROWS):
        pv[1 + r, C0 - 1 : C0, :] = first[r : r + 1, :]
        pv[1 + r, C0 + COLS : C0 + COLS + 1, :] = last[r : r + 1, :]

    def ahead(v):
        return pltpu.roll(v, DEPTH - 1, 1)

    def behind(v):
        return pltpu.roll(v, 1, 1)

    top, bottom = lane16 == DEPTH - 1, lane16 == 0

    for r in range(ROWS):
        e = pv[1 + r, C0 : C0 + COLS, :]
        near = (
            pv[r, C0 : C0 + COLS, :],
            pv[2 + r, C0 : C0 + COLS, :],
            pv[1 + r, C0 - 1 : C0 - 1 + COLS, :],
            pv[1 + r, C0 + 1 : C0 + 1 + COLS, :],
            jnp.where(bottom, e, behind(e)),
            jnp.where(top, e, ahead(e)),
        )
        dsum = jnp.zeros_like(e)
        faces = []
        for k, o in enumerate(near):
            f = 2.0 * e * o / (e + o)
            face[k, r] = f
            faces.append(f)
            dsum = dsum + f
        half = 0.5 / dsum
        coef[r] = half
        se = jnp.sqrt(e)
        six = SIX * se
        root[0, r] = se
        root[1, r] = six
        root[2, r] = 1.0 / se
        at = slice(r * COLS, (r + 1) * COLS)
        for a in range(3):
            w = rhs[a, r] * six
            force[a, r] = w
            x = half * w
            xs[0, a, 1 + r, C0 : C0 + COLS, :] = x
            nat[0, a, at, :] = x * six
        w = -0.5 * (rhs[3, r] * se)
        force[3, r] = w
        xs[0, 3, 1 + r, C0 : C0 + COLS, :] = w
        nat[0, 3, at, :] = -0.5 * rhs[3, r]
        nat[2, 0, at, :] = half * jnp.where(i == 0, faces[0], faces[1])
        nat[2, 1, at, :] = half * jnp.where(j == 0, faces[2], faces[3])
        nat[2, 2, at, :] = (0.5 * SIX) * (e * half)

    def sweep(n, out_at):
        for r in range(ROWS):
            def get(a, dr, dc):
                return xs[n, a, 1 + r + dr, C0 + dc : C0 + dc + COLS, :]

            e = pv[1 + r, C0 : C0 + COLS, :]
            half = coef[r]
            around = []
            for a in range(4):
                v = get(a, 0, 0)
                around.append(
                    (
                        get(a, -1, 0),
                        get(a, 1, 0),
                        get(a, 0, -1),
                        get(a, 0, 1),
                        jnp.where(bottom, 0.0, behind(v)),
                        jnp.where(top, 0.0, ahead(v)),
                        v,
                    )
                )
            pr = around[3]
            div = jnp.zeros_like(e)
            for a in range(3):
                total = force[a, r] - 0.5 * (pr[2 * a + 1] - pr[2 * a])
                for k in range(6):
                    total = total + face[k, r] * around[a][k]
                x = 0.5 * around[a][6] + half * total
                out_at(a, r, x)
                div = div + (around[a][2 * a + 1] - around[a][2 * a])
            out_at(3, r, 0.5 * pr[6] + force[3, r] - 0.25 * (e * div))

    def to_state(a, r, v):
        return v * (root[2, r] if a == 3 else root[1, r])

    def pack(n, field, where):
        t = nat[n, field].T
        for w in where:
            for d in range(4):
                tb[n, pl.ds(4 * w + d, LON, stride=PIECE), :] = t[LON * d : LON * (d + 1), :]

    def piece(n, jj):
        return tb.at[n, pl.ds(pl.multiple_of(jj * PIECE, PIECE), PIECE)]

    def start_phase_1(n):
        for a in range(4):
            pack(n, a, (a,))
        to_row(
            0,
            lambda jj: copy_to(piece(n, jj), r1.at[n, j], sem_1.at[n, 0], sem_1.at[n, 1], at_lon(jj)),
        )
        r1[n, pl.ds(j, 1)] = tb[n, pl.ds(pl.multiple_of(j * PIECE, PIECE), PIECE), :][None]

    def start_halo(n):
        for a in range(4):
            h_srow[n, 0, a] = xs[n, a, 1, C0 : C0 + COLS, :]
            h_srow[n, 1, a] = xs[n, a, ROWS, C0 : C0 + COLS, :]
            for r in range(ROWS):
                h_scol[n, 0, a, r : r + 1, :] = xs[n, a, 1 + r, C0 : C0 + 1, :]
                h_scol[n, 1, a, r : r + 1, :] = xs[n, a, 1 + r, C0 + COLS - 1 : C0 + COLS, :]
        copy_to(h_srow.at[n, 0], h_row.at[n, 1], sem_h.at[n, 0], sem_h.at[n, 1], at_lat(south))
        copy_to(h_srow.at[n, 1], h_row.at[n, 0], sem_h.at[n, 0], sem_h.at[n, 1], at_lat(north))
        copy_to(h_scol.at[n, 0], h_col.at[n, 1], sem_h.at[n, 3], sem_h.at[n, 2], at_lon(west))
        copy_to(h_scol.at[n, 1], h_col.at[n, 0], sem_h.at[n, 3], sem_h.at[n, 2], at_lon(east))

    SIDES_LAT = ((0, 0, 0, 0), (1, LAT - 1, ROWS - 1, ROWS + 1))
    SIDES_LON = ((0, 0, 0, C0 - 1), (1, LON - 1, COLS - 1, C0 + COLS))

    def fill_halo(n):
        take_bytes(h_row.at[n], sem_h.at[n, 1])
        take_bytes(h_col.at[n], sem_h.at[n, 2])
        for side, edge, r_in, r_out in SIDES_LAT:
            for a in range(4):
                xs[n, a, r_out, C0 : C0 + COLS, :] = jnp.where(i == edge, 0.0, h_row[n, side, a])
        for side, edge, c_in, c_out in SIDES_LON:
            for a in range(4):
                v = jnp.where(j == edge, 0.0, h_col[n, side, a])
                for r in range(ROWS):
                    xs[n, a, 1 + r, c_out : c_out + 1, :] = v[r : r + 1, :]

    start_phase_1(0)
    start_halo(0)

    take_bytes(metas.at[pl.ds(0, LON - 1)], sem_m.at[1])
    total = jnp.zeros((8, 128), I32)
    for c in range(LON):
        total = total + metas[c]
    own = jnp.where(lane8 % 4 == 1, total, 0)
    own = pltpu.roll(own, 127, 1) + own + pltpu.roll(own, 1, 1) + pltpu.roll(own, 2, 1)
    bases[...] = own

    def send_bases(o, c):
        copy_to(bases, other_bases.at[i], sem_b.at[0], sem_b.at[1], across(o))
        return c

    lax.fori_loop(0, LAT, send_bases, 0)

    to_row(0, lambda jj: copy_to(info, infos.at[j], sem_i.at[0], sem_i.at[1], at_lon(jj)))

    @pl.when(is_edge)
    def _():
        pack(2, 0, (0, 1))
        pack(2, 2, (2,))
        pack(2, 1, (3,))
        to_row(0, lambda jj: copy_to(piece(2, jj), rc.at[j], sem_c.at[0], sem_c.at[1], at_lon(jj)))
        rc[pl.ds(j, 1)] = tb[2, pl.ds(pl.multiple_of(j * PIECE, PIECE), PIECE), :][None]

    fill_halo(0)

    def second(a, r, v):
        xs[1, a, 1 + r, C0 : C0 + COLS, :] = v

    def second_early(a, r, v):
        second(a, r, v)
        nat[1, a, r * COLS : (r + 1) * COLS, :] = to_state(a, r, v)

    sweep(0, second_early)
    start_phase_1(1)

    take_bytes(other_bases, sem_b.at[1])
    base = jnp.zeros((8, 128), I32)
    for r in range(LAT):
        base = base + jnp.where(sub8 == r, other_bases[r], 0)
    col = base & (LON - 1)
    offset = (lane8 & 1) + COLS * ((lane8 // 2) & 1)
    pick = []
    for t in range(2):
        a = jnp.zeros((8, 128), I32)
        for c in range(LON):
            a = a + jnp.where(col + t == c, metas[c], 0)
        a = jnp.where(lane8 % 4 == 0, a, 0)
        pick.append(a + pltpu.roll(a, 1, 1) + pltpu.roll(a, 2, 1) + pltpu.roll(a, 3, 1) + offset)

    def inner(v):
        w = jnp.zeros((8, 128), I32)
        for r in range(1, LAT - 1):
            here = jnp.logical_and(lane8 >= 8 * r - 4, lane8 < 8 * r + 4)
            row = jnp.broadcast_to(v[r : r + 1, :], (8, 128))
            w = w + jnp.where(here, pltpu.roll(row, 8 * r, 1), 0)
        return w[0:1]

    groups = []
    for g in range(3):
        def of(v):
            row = inner(v) if g == 2 else v[7 * g : 7 * g + 1, :]
            return jnp.broadcast_to(row, (PIECE, 128))
        groups.append((of(col), of(pick[0]), of(pick[1])))

    own_row = own >> 5
    packed_row = jnp.where(lane8 < 64, pltpu.roll(own_row, 8 * i, 1), pltpu.roll(own_row, 8 * i + 64, 1))
    rows_full = jnp.broadcast_to(own_row[0:1], (PIECE, 128))
    rows_packed = jnp.broadcast_to(packed_row[0:1], (PIECE, 128))

    def lanes_at(v, index):
        return jnp.take_along_axis(v, index, axis=1, mode="promise_in_bounds")

    def phase_2(n):
        picked = []
        for g in range(3):
            at_col, first, second = groups[g]
            for t in range(2):
                index = second if t else first
                acc = jnp.zeros((PIECE, 128), F32)
                for c in range(LON):
                    acc = jnp.where(at_col == c - t, lanes_at(r1[n, c], index), acc)
                picked.append(acc)
            if g < 2:
                for t in range(2):
                    xb[n, g, t] = picked[2 * g + t]
                copy_to(
                    xb.at[n, g], xr.at[n, i], sem_2.at[n, 0], sem_2.at[n, 1], across((LAT - 1) * g)
                )
        xbi[n] = jnp.where(lane16 < 64, picked[4], pltpu.roll(picked[5], 64, 1))

        def send_inner(o, c):
            copy_to(xbi.at[n], xr.at[n, i, 0], sem_2.at[n, 2], sem_2.at[n, 1], across(o))
            return c

        lax.fori_loop(1, LAT - 1, send_inner, 0)

    def pick_rows(n):
        @pl.when(lat_edge)
        def _():
            take_bytes(xr.at[n], sem_2.at[n, 1])
            for s in range(2):
                for t in range(2):
                    acc = jnp.zeros((PIECE, 128), F32)
                    for r in range(LAT):
                        acc = jnp.where(rows_full + s == r, xr[n, r, t], acc)
                    ys[n, s, t] = acc

        @pl.when(jnp.logical_not(lat_edge))
        def _():
            take_bytes(xr.at[n, :, 0], sem_2.at[n, 1])
            for s in range(2):
                acc = jnp.zeros((PIECE, 128), F32)
                for r in range(LAT):
                    acc = jnp.where(rows_packed + s == r, xr[n, r, 0], acc)
                ys[n, s, 0] = pltpu.roll(acc, lax.rem(128 - 8 * i, 128), 1)
                ys[n, s, 1] = pltpu.roll(acc, 64 - 8 * i, 1)

    def phase_3(n):
        z = jnp.concatenate([ys[n, 0, 0], ys[n, 1, 0], ys[n, 0, 1], ys[n, 1, 1]], axis=0)
        z = jnp.concatenate([z, z], axis=0).T
        for jj in range(LON):
            zb[n, jj] = z[4 * jj : 4 * jj + 4, :]

        def send(jj):
            copy_to(zb.at[n, jj], dd.at[n, j], sem_3.at[n, 0], sem_3.at[n, 1], at_lon(jj))

        @pl.when(lat_edge)
        def _():
            to_row(0, send)

        @pl.when(jnp.logical_not(lat_edge))
        def _():
            @pl.when(j != 0)
            def _():
                send(0)

            @pl.when(j != LON - 1)
            def _():
                send(LON - 1)

    def ghost_columns(n):
        dd[n, pl.ds(j, 1)] = zb[n, pl.ds(j, 1)]
        take_bytes(dd.at[n, pl.ds(0, LON - 1)], sem_3.at[n, 1])
        lane32 = iota((LON, 128), 1)
        for h in range(2):
            both = jnp.where(lane32 < 64, dd[n, :, 2 * h, :], pltpu.roll(dd[n, :, 2 * h + 1, :], 64, 1))
            turned[128 * h : 128 * (h + 1), :] = jnp.concatenate([both] * 4, axis=0).T
        g = []
        for a in range(4):
            cells_at = jnp.zeros((16, 128), F32)
            for d in range(4):
                v = turned[pl.ds(4 * a + d, 16, stride=16), :]
                cells_at = jnp.where(lane16 // LON == d, v, cells_at)
            g.append(
                lax.dot_general(
                    mix, cells_at, (((1,), (0,)), ((), ())),
                    precision=lax.Precision.HIGHEST, preferred_element_type=F32,
                )
            )
        ghost[0] = cosine * g[0] - sine * g[1]
        ghost[1] = sine * g[0] + cosine * g[1]
        ghost[2] = g[2]
        ghost[3] = g[3]
        for side, edge, r_in, r_out in SIDES_LAT:
            @pl.when(i == edge)
            def _():
                for a in range(4):
                    v = ghost[a, side * COLS : (side + 1) * COLS, :]
                    v = v * root[0, r_in] if a == 3 else v / root[1, r_in]
                    xs[n, a, r_out, C0 : C0 + COLS, :] = v

        for side, edge, c_in, c_out in SIDES_LON:
            @pl.when(j == edge)
            def _():
                at = 2 * COLS + side * ROWS
                for a in range(4):
                    for r in range(ROWS):
                        v = ghost[a, at + r : at + r + 1, :]
                        if a == 3:
                            v = v * root[0, r, c_in : c_in + 1, :]
                        else:
                            v = v / root[1, r, c_in : c_in + 1, :]
                        xs[n, a, 1 + r, c_out : c_out + 1, :] = v

    take_bytes(r1.at[0, pl.ds(0, LON - 1)], sem_1.at[0, 1])
    phase_2(0)

    take_bytes(infos.at[pl.ds(0, LON - 1)], sem_i.at[1])

    @pl.when(lat_edge)
    def _():
        start = jnp.where(i == 0, 0, COLS)
        for b in range(4):
            rows = []
            for f in range(7):
                v = lanes_at(infos[8 * b : 8 * b + 8, f, :], start + lane8 % COLS)
                rows.append(jnp.sum(jnp.where(lane8 // COLS == sub8, v, 0.0), axis=0, keepdims=True))
            for k in range(4):
                for t in range(2):
                    for s in range(2):
                        m = 4 * (4 * k + 2 * t + s) + b
                        wv[m : m + 1, :] = jnp.where(rows[6] == t + 2.0 * s, rows[k], 0.0)
            wv[64 + b : 65 + b, :] = rows[4]
            wv[68 + b : 69 + b, :] = rows[5]

    for side, c in ((0, 0), (1, LON - 1)):
        own_lane = lane8 % COLS == (COLS - 1) * side
        v = lanes_at(infos[c], 2 * COLS + ROWS * side + lane8 // COLS)
        v = jnp.where(own_lane, v, 0.0)
        for k in range(4):
            for t in range(2):
                for s in range(2):
                    m = 4 * k + 2 * t + s
                    ww[side, m : m + 1, :] = jnp.where(v[6:7] == t + 2.0 * s, v[k : k + 1], 0.0)
        ww[side, 16:17, :] = v[4:5]
        ww[side, 17:18, :] = v[5:6]

    def swap(v):
        return pltpu.roll(v, 4, 0)

    def rotated(g, cos, sin):
        return cos * g + jnp.where(low8, -sin, sin) * swap(g)

    pick_rows(0)
    take_bytes(r1.at[1, pl.ds(0, LON - 1)], sem_1.at[1, 1])

    @pl.when(lat_edge)
    def _():
        take_bytes(rc.at[pl.ds(0, LON - 1)], sem_c.at[1])
        sign = jnp.where(i == 0, 1.0, -1.0)
        start = jnp.where(i == 0, 0, 128 - COLS)
        here = jnp.logical_and(lane8 >= start, lane8 < start + COLS)
        for b in range(4):
            index = 4 * (8 * b + lane16 // COLS)
            g = jnp.zeros((PIECE, 128), F32)
            for k in range(4):
                for t in range(2):
                    for s in range(2):
                        m = 4 * (4 * k + 2 * t + s) + b
                        g = g + lanes_at(ys[0, s, t], index + k) * wv[m : m + 1, :]
            g0 = rotated(g[0:8], wv[64 + b : 65 + b, :], wv[68 + b : 69 + b, :])
            g1 = g[8:16]
            for o in range(8):
                c = 8 * b + o
                shift = lax.rem(start + 128 - COLS * o, 128)
                u = jnp.where(here, pltpu.roll(g0, shift, 1), 0.0)
                w = jnp.where(here, pltpu.roll(g1, shift, 1), 0.0)
                fc, bc = rc[c, 0:8, :], rc[c, 8:16, :]
                r1[1, c, 0:8, :] = r1[1, c, 0:8, :] + (fc * u + jnp.where(low8, sign * bc * swap(w), 0.0))
                r1[1, c, 8:16, :] = r1[1, c, 8:16, :] + jnp.where(low8, fc * w, (sign * THIRD) * swap(u))

    @pl.when(jnp.logical_not(lat_edge))
    def _():
        @pl.when(lon_edge)
        def _():
            take_bytes(rc.at[0], sem_c.at[1])

        @pl.when(jnp.logical_not(lon_edge))
        def _():
            take_bytes(rc.at[pl.ds(0, 2)], sem_c.at[1])

    for side, c in ((0, 0), (1, LON - 1)):
        sign = 1.0 - 2.0 * side
        g = jnp.zeros((PIECE, 128), F32)
        for k in range(4):
            for t in range(2):
                for s in range(2):
                    m = 4 * k + 2 * t + s
                    g = g + ys[0, s, t, :, 4 * c + k : 4 * c + k + 1] * ww[side, m : m + 1, :]
        u = rotated(g[0:8], ww[side, 16:17, :], ww[side, 17:18, :])
        w = g[8:16]
        bc = rc[c, 8:16, :]
        cb = swap(bc)
        fc = jnp.where(low8, cb, bc)
        r1[1, c, 0:8, :] = r1[1, c, 0:8, :] + (fc * u + jnp.where(low8, 0.0, sign * cb * w))
        r1[1, c, 8:16, :] = r1[1, c, 8:16, :] + jnp.where(low8, fc * w, (sign * THIRD) * u)

    phase_2(1)

    phase_3(0)

    @pl.when(is_edge)
    def _():
        ghost_columns(0)
        sweep(0, second)

    start_halo(1)
    fill_halo(1)
    pick_rows(1)
    phase_3(1)

    @pl.when(is_edge)
    def _():
        ghost_columns(1)

    def third(a, r, v):
        out[a, r] = to_state(a, r, v)

    sweep(1, third)

    take_bytes(hv_row, sem_hv.at[0])
    take_bytes(hv_col, sem_hv.at[3])
    take_bytes(metas.at[pl.ds(0, LON - 1)], sem_m.at[0])
    take_bytes(infos.at[pl.ds(0, LON - 1)], sem_i.at[0])
    take_bytes(other_bases, sem_b.at[0])

    @pl.when(is_edge)
    def _():
        take_bytes(rc.at[pl.ds(0, LON - 1)], sem_c.at[0])

    for n in range(2):
        take_bytes(h_row.at[n], sem_h.at[n, 0])
        take_bytes(h_col.at[n], sem_h.at[n, 3])
        take_bytes(r1.at[n, pl.ds(0, LON - 1)], sem_1.at[n, 0])
        take_bytes(xb.at[n], sem_2.at[n, 0])
        take_bytes(r1.at[n, pl.ds(0, LAT - 2)], sem_2.at[n, 2])

        @pl.when(lat_edge)
        def _():
            take_bytes(dd.at[n, pl.ds(0, LON - 1)], sem_3.at[n, 0])

        @pl.when(jnp.logical_not(lat_edge))
        def _():
            @pl.when(lon_edge)
            def _():
                take_bytes(dd.at[n, 0], sem_3.at[n, 0])

            @pl.when(jnp.logical_not(lon_edge))
            def _():
                take_bytes(dd.at[n, pl.ds(0, 2)], sem_3.at[n, 0])


def body(viscosity, forcing, send_cell, partner, ghost_src, ghost_weight, ghost_angle):
    dma = pltpu.SemaphoreType.DMA
    pad = ((0, 0), (0, 128 - GHOSTS))

    def floats(*shape):
        return pltpu.VMEM(shape, F32)

    def ints(*shape):
        return pltpu.VMEM(shape, I32)

    scratch = [
        floats(ROWS, COLS, DEPTH),
        floats(4, ROWS, COLS, DEPTH),
        ints(8, 128),
        ints(8, 128),
        ints(1, 128),
        floats(1, 128),
        floats(GHOSTS, 4),
        floats(ROWS + 2, C0 + COLS + 8, DEPTH),
        floats(2, COLS, DEPTH),
        floats(2, ROWS, DEPTH),
        floats(2, COLS, DEPTH),
        floats(2, ROWS, DEPTH),
        floats(2, 4, ROWS + 2, C0 + COLS + 8, DEPTH),
        floats(6, ROWS, COLS, DEPTH),
        floats(ROWS, COLS, DEPTH),
        floats(4, ROWS, COLS, DEPTH),
        floats(3, ROWS, COLS, DEPTH),
        floats(2, 2, 4, COLS, DEPTH),
        floats(2, 2, 4, ROWS, DEPTH),
        floats(2, 2, 4, COLS, DEPTH),
        floats(2, 2, 4, ROWS, DEPTH),
        ints(8, 128),
        ints(LON, 8, 128),
        ints(8, 128),
        ints(LAT, 8, 128),
        floats(8, 128),
        floats(LON, 8, 128),
        floats(128, 128),
        floats(3, 4, CELLS, DEPTH),
        floats(3, LON * PIECE, CELLS),
        floats(2, LON, PIECE, CELLS),
        floats(LON, PIECE, CELLS),
        floats(2, 2, 2, PIECE, 128),
        floats(2, PIECE, 128),
        floats(2, LAT, 2, PIECE, 128),
        floats(2, 2, 2, PIECE, 128),
        floats(2, LON, 4, 128),
        floats(2, LON, 4, 128),
        floats(256, 128),
        floats(4, GHOSTS, DEPTH),
        floats(72, 128),
        floats(2, 24, 128),
        dma((7,)), dma((4,)), dma((2,)), dma((2,)), dma((2,)), dma((2, 4)), dma((2, 2)), dma((2,)),
        dma((2, 3)), dma((2, 2)),
    ]
    state = pl.pallas_call(
        kernel,
        out_shape=jax.ShapeDtypeStruct((4, ROWS, COLS, DEPTH), F32),
        in_specs=[pl.BlockSpec(memory_space=pl.ANY)] * 7,
        out_specs=pl.BlockSpec(memory_space=pltpu.VMEM),
        scratch_shapes=scratch,
        compiler_params=pltpu.CompilerParams(
            collective_id=0, has_side_effects=True, vmem_limit_bytes=32 << 20
        ),
    )(
        viscosity.reshape(ROWS, COLS, DEPTH),
        forcing.reshape(4, ROWS, COLS, DEPTH),
        send_cell.reshape(LAT, 4 * LON),
        jnp.broadcast_to(partner.reshape(4)[0], (8, 128)),
        jnp.pad(ghost_src.reshape(1, GHOSTS), pad),
        jnp.pad(ghost_angle.reshape(1, GHOSTS), pad),
        ghost_weight.reshape(GHOSTS, 4),
    )
    return state[:, None]


def solution(mesh):
    placed = (
        P("panel", "lat", "lon", None),
        P(None, "panel", "lat", "lon", None),
        P("panel", "lat", "lon", None),
        P("panel", "lat", "lon", None),
        P("panel", "lat", "lon", None),
        P("panel", "lat", "lon", None, None),
        P("panel", "lat", "lon", None),
    )
    return jax.shard_map(
        body,
        mesh=mesh,
        in_specs=placed,
        out_specs=P(None, "panel", "lat", "lon", None),
        check_vma=False,
    )
```

```python
import math

import jax
import jax.numpy as jnp
from jax import lax
from jax.experimental import pallas as pl
from jax.experimental.pallas import tpu as pltpu
from jax.sharding import PartitionSpec as P

MESH = pl.DeviceIdType.MESH
LAT, LON = 8, 32
ROWS, COLS, DEPTH = 8, 16, 128
CELLS = ROWS * COLS
GHOSTS = 48
PIECE = 4 * DEPTH // LON
C0 = 8
F32, I32 = jnp.float32, jnp.int32
SIX = math.sqrt(6.0)
THIRD = 0.25 / SIX


def copy_to(src, dst, send, recv, device):
    pltpu.make_async_remote_copy(
        src_ref=src,
        dst_ref=dst,
        send_sem=send,
        recv_sem=recv,
        device_id=device,
        device_id_type=MESH,
    ).start()


def take_bytes(ref, sem):
    pltpu.make_async_copy(ref, ref, sem).wait()


def iota(shape, dim):
    return lax.broadcasted_iota(I32, shape, dim)


def kernel(
    visc_in, rhs_in, cells_in, partner_in, src_in, angle_in, weight_in, out,
    visc, rhs, cells, partner, src, angle, weight,
    pv, hv_row, hv_col, hv_srow, hv_scol,
    xs, face, coef, force, root,
    h_srow, h_scol, h_row, h_col,
    meta, metas, row_metas, bases, other_bases, row_bases, info, square,
    nat, tb, r1, own_edge, edges, row_edges, xb, xbi, xr, ys, zb, dd, turned, ghost, wv, ww, cv, cw,
    sem_in, sem_hv, sem_m, sem_b, sem_h, sem_1, sem_c, sem_2, sem_3,
):
    p = lax.axis_index("panel")
    i = lax.axis_index("lat")
    j = lax.axis_index("lon")
    q = 1 - p
    lat_edge = jnp.logical_or(i == 0, i == LAT - 1)
    lon_edge = jnp.logical_or(j == 0, j == LON - 1)
    is_edge = jnp.logical_or(lat_edge, lon_edge)

    def at_lon(jj):
        return {"panel": p, "lat": i, "lon": jj}

    def at_lat(ii):
        return {"panel": p, "lat": ii, "lon": j}

    def across(ii):
        return {"panel": q, "lat": ii, "lon": j}

    south, north = lax.rem(i + LAT - 1, LAT), lax.rem(i + 1, LAT)
    west, east = lax.rem(j + LON - 1, LON), lax.rem(j + 1, LON)

    def to_row(n, send):
        def step(o, c):
            send(lax.rem(j + o, LON))
            return c

        lax.fori_loop(1, LON, step, 0)

    barrier = pltpu.get_barrier_semaphore()

    def greet(device):
        pl.semaphore_signal(barrier, 1, device_id=device, device_id_type=MESH)

    def greet_across(o, c):
        greet(across(o))
        return c

    lax.fori_loop(0, LAT, greet_across, 0)
    greet(at_lat(south))
    greet(at_lat(north))
    to_row(0, lambda jj: greet(at_lon(jj)))

    moves = [
        pltpu.make_async_copy(a, b, sem_in.at[n])
        for n, (a, b) in enumerate(
            (
                (visc_in, visc), (cells_in, cells), (partner_in, partner), (weight_in, weight),
                (src_in, src), (angle_in, angle), (rhs_in, rhs),
            )
        )
    ]
    for move in moves:
        move.start()
    for move in moves:
        move.wait()
    sub8 = iota((8, 128), 0)
    lane8 = iota((8, 128), 1)
    lane16 = iota((16, 128), 1)
    low8 = sub8 < 4

    def lanes_at(v, index):
        return jnp.take_along_axis(v, index, axis=1, mode="promise_in_bounds")

    def fold(v):
        for h in (4, 2, 1):
            v = v + pltpu.roll(v, h, 0)
        return v

    receiver_row = jnp.where(lane8 < 32, 0, jnp.where(lane8 < 64, LAT - 1, (lane8 - 64) // 2))
    at_row = sub8 == receiver_row
    asked = lanes_at(cells[...], jnp.where(lane8 < 64, 4 * (lane8 % 32), 124 * (lane8 % 2)))
    asked = fold(jnp.where(at_row, asked, 0))
    my_base = jnp.broadcast_to(partner[0:1, 0:1], (8, 128))
    asked = jnp.where(lane8 < 96, asked, jnp.where(lane8 == 96 + j, my_base, 0))
    meta[...] = asked[0:1]
    metas[pl.ds(j, 1)] = meta[...][None]
    hv_srow[0] = visc[0]
    hv_srow[1] = visc[ROWS - 1]
    for r in range(ROWS):
        hv_scol[0, r : r + 1, :] = visc[r, 0:1, :]
        hv_scol[1, r : r + 1, :] = visc[r, COLS - 1 : COLS, :]
    pv[1 : ROWS + 1, C0 : C0 + COLS, :] = visc[...]

    info[...] = jnp.zeros((8, 128), F32)
    info[0:4, 0:GHOSTS] = weight[...] / jnp.sum(weight[...], axis=0, keepdims=True)
    info[4:5, 0:GHOSTS] = jnp.cos(angle[...])
    info[5:6, 0:GHOSTS] = jnp.sin(angle[...])
    info[6:7, 0:GHOSTS] = src[...].astype(F32)
    square[...] = jnp.zeros((128, 128), F32)
    square[0:8, :] = info[...]
    columns = square[...].T[0:GHOSTS]

    def column(k):
        return jnp.broadcast_to(columns[:, k : k + 1], (GHOSTS, 128))

    cosine = column(4)
    sine = column(5)
    lane48 = iota((GHOSTS, 128), 1)
    mix = jnp.zeros((GHOSTS, 128), F32)
    for k in range(4):
        mix = mix + jnp.where(lane48 // 4 == k, column(k), 0.0)
    which = (lane48 // 2 % 2 + 2 * (lane48 % 2)).astype(F32)
    mix = jnp.where(which == column(6), mix, 0.0)[:, 0:16]

    pl.semaphore_wait(barrier, LAT + 2 + LON - 1)

    copy_to(hv_srow.at[0], hv_row.at[1], sem_hv.at[0], sem_hv.at[1], at_lat(south))
    copy_to(hv_srow.at[1], hv_row.at[0], sem_hv.at[0], sem_hv.at[1], at_lat(north))
    copy_to(hv_scol.at[0], hv_col.at[1], sem_hv.at[3], sem_hv.at[2], at_lon(west))
    copy_to(hv_scol.at[1], hv_col.at[0], sem_hv.at[3], sem_hv.at[2], at_lon(east))
    to_row(0, lambda jj: copy_to(meta, metas.at[j], sem_m.at[0], sem_m.at[1], at_lon(jj)))

    take_bytes(hv_row, sem_hv.at[1])
    take_bytes(hv_col, sem_hv.at[2])
    pv[0, C0 : C0 + COLS, :] = jnp.where(i == 0, visc[0], hv_row[0])
    pv[ROWS + 1, C0 : C0 + COLS, :] = jnp.where(i == LAT - 1, visc[ROWS - 1], hv_row[1])
    first = jnp.where(j == 0, hv_scol[0], hv_col[0])
    last = jnp.where(j == LON - 1, hv_scol[1], hv_col[1])
    for r in range(ROWS):
        pv[1 + r, C0 - 1 : C0, :] = first[r : r + 1, :]
        pv[1 + r, C0 + COLS : C0 + COLS + 1, :] = last[r : r + 1, :]

    def ahead(v):
        return pltpu.roll(v, DEPTH - 1, 1)

    def behind(v):
        return pltpu.roll(v, 1, 1)

    top, bottom = lane16 == DEPTH - 1, lane16 == 0

    for r in range(ROWS):
        e = pv[1 + r, C0 : C0 + COLS, :]
        near = (
            pv[r, C0 : C0 + COLS, :],
            pv[2 + r, C0 : C0 + COLS, :],
            pv[1 + r, C0 - 1 : C0 - 1 + COLS, :],
            pv[1 + r, C0 + 1 : C0 + 1 + COLS, :],
            jnp.where(bottom, e, behind(e)),
            jnp.where(top, e, ahead(e)),
        )
        dsum = jnp.zeros_like(e)
        for k, o in enumerate(near):
            f = 2.0 * e * o / (e + o)
            face[k, r] = f
            dsum = dsum + f
        half = 0.5 / dsum
        coef[r] = half
        se = jnp.sqrt(e)
        six = SIX * se
        root[0, r] = se
        root[1, r] = six
        root[2, r] = 1.0 / se
        at = slice(r * COLS, (r + 1) * COLS)
        for a in range(3):
            w = rhs[a, r] * six
            force[a, r] = w
            x = half * w
            xs[0, a, 1 + r, C0 : C0 + COLS, :] = x
            nat[0, a, at, :] = x * six
        w = -0.5 * (rhs[3, r] * se)
        force[3, r] = w
        xs[0, 3, 1 + r, C0 : C0 + COLS, :] = w
        nat[0, 3, at, :] = -0.5 * rhs[3, r]

    def sweep(n, out_at):
        for r in range(ROWS):
            def get(a, dr, dc):
                return xs[n, a, 1 + r + dr, C0 + dc : C0 + dc + COLS, :]

            e = pv[1 + r, C0 : C0 + COLS, :]
            half = coef[r]
            around = []
            for a in range(4):
                v = get(a, 0, 0)
                around.append(
                    (
                        get(a, -1, 0),
                        get(a, 1, 0),
                        get(a, 0, -1),
                        get(a, 0, 1),
                        jnp.where(bottom, 0.0, behind(v)),
                        jnp.where(top, 0.0, ahead(v)),
                        v,
                    )
                )
            pr = around[3]
            div = jnp.zeros_like(e)
            for a in range(3):
                total = force[a, r] - 0.5 * (pr[2 * a + 1] - pr[2 * a])
                for k in range(6):
                    total = total + face[k, r] * around[a][k]
                x = 0.5 * around[a][6] + half * total
                out_at(a, r, x)
                div = div + (around[a][2 * a + 1] - around[a][2 * a])
            out_at(3, r, 0.5 * pr[6] + force[3, r] - 0.25 * (e * div))

    def to_state(a, r, v):
        return v * (root[2, r] if a == 3 else root[1, r])

    def pack(n, field, where):
        t = nat[n, field].T
        for w in where:
            for d in range(4):
                tb[n, pl.ds(4 * w + d, LON, stride=PIECE), :] = t[LON * d : LON * (d + 1), :]

    def piece(n, jj):
        return tb.at[n, pl.ds(pl.multiple_of(jj * PIECE, PIECE), PIECE)]

    def start_phase_1(n):
        for a in range(4):
            pack(n, a, (a,))
        to_row(
            0,
            lambda jj: copy_to(piece(n, jj), r1.at[n, j], sem_1.at[n, 0], sem_1.at[n, 1], at_lon(jj)),
        )
        r1[n, pl.ds(j, 1)] = tb[n, pl.ds(pl.multiple_of(j * PIECE, PIECE), PIECE), :][None]

    def start_halo(n):
        for a in range(4):
            h_srow[n, 0, a] = xs[n, a, 1, C0 : C0 + COLS, :]
            h_srow[n, 1, a] = xs[n, a, ROWS, C0 : C0 + COLS, :]
            for r in range(ROWS):
                h_scol[n, 0, a, r : r + 1, :] = xs[n, a, 1 + r, C0 : C0 + 1, :]
                h_scol[n, 1, a, r : r + 1, :] = xs[n, a, 1 + r, C0 + COLS - 1 : C0 + COLS, :]
        copy_to(h_srow.at[n, 0], h_row.at[n, 1], sem_h.at[n, 0], sem_h.at[n, 1], at_lat(south))
        copy_to(h_srow.at[n, 1], h_row.at[n, 0], sem_h.at[n, 0], sem_h.at[n, 1], at_lat(north))
        copy_to(h_scol.at[n, 0], h_col.at[n, 1], sem_h.at[n, 3], sem_h.at[n, 2], at_lon(west))
        copy_to(h_scol.at[n, 1], h_col.at[n, 0], sem_h.at[n, 3], sem_h.at[n, 2], at_lon(east))

    SIDES_LAT = ((0, 0, 0, 0), (1, LAT - 1, ROWS - 1, ROWS + 1))
    SIDES_LON = ((0, 0, 0, C0 - 1), (1, LON - 1, COLS - 1, C0 + COLS))

    def fill_halo(n):
        take_bytes(h_row.at[n], sem_h.at[n, 1])
        take_bytes(h_col.at[n], sem_h.at[n, 2])
        for side, edge, r_in, r_out in SIDES_LAT:
            for a in range(4):
                xs[n, a, r_out, C0 : C0 + COLS, :] = jnp.where(i == edge, 0.0, h_row[n, side, a])
        for side, edge, c_in, c_out in SIDES_LON:
            for a in range(4):
                v = jnp.where(j == edge, 0.0, h_col[n, side, a])
                for r in range(ROWS):
                    xs[n, a, 1 + r, c_out : c_out + 1, :] = v[r : r + 1, :]

    start_phase_1(0)
    start_halo(0)

    take_bytes(metas.at[pl.ds(0, LON - 1)], sem_m.at[1])
    for c in range(LON):
        row_metas[c : c + 1, :] = metas[c]
    total = row_metas[0:8] + row_metas[8:16] + row_metas[16:24] + row_metas[24:32]
    total = jnp.where(lane8 < 96, 0, fold(total))
    bases[...] = total[0:1]

    def send_bases(o, c):
        copy_to(bases, other_bases.at[i], sem_b.at[0], sem_b.at[1], across(o))
        return c

    lax.fori_loop(0, LAT, send_bases, 0)

    @pl.when(is_edge)
    def _():
        def pressure(r):
            return (0.5 * SIX) * (pv[1 + r, C0 : C0 + COLS, :] * coef[r])

        low = i == 0
        square[...] = jnp.zeros((128, 128), F32)
        square[0:COLS, :] = jnp.where(low, coef[0] * face[0, 0], coef[ROWS - 1] * face[1, ROWS - 1])
        square[COLS : 2 * COLS, :] = jnp.where(low, pressure(0), pressure(ROWS - 1))
        for r in range(ROWS):
            at = 2 * COLS + r
            f = jnp.where(
                j == 0,
                coef[r, 0:1, :] * face[2, r, 0:1, :],
                coef[r, COLS - 1 : COLS, :] * face[3, r, COLS - 1 : COLS, :],
            )
            b = pressure(r)
            square[at : at + 1, :] = f
            square[at + ROWS : at + ROWS + 1, :] = jnp.where(j == 0, b[0:1], b[COLS - 1 : COLS])
        turn = square[...].T
        lane32 = iota((LON, 128), 1)
        first = jnp.zeros((LON, 128), F32)
        second = jnp.zeros((LON, 128), F32)
        for d in range(4):
            slab = turn[LON * d : LON * (d + 1), :]
            v = pltpu.roll(slab, LON * d, 1) if d else slab
            first = jnp.where(lane32 // LON == d, v, first)
            second = jnp.where(lane32 // LON == d, pltpu.roll(slab, (LON * d + 96) % 128, 1), second)
        mine = []
        for at in (jnp.where(low, 0, COLS), 2 * COLS + jnp.where(j == 0, 0, ROWS)):
            v = lanes_at(info[...], at + lane8 % COLS)
            mine.append(fold(jnp.where(lane8 // COLS == sub8, v, 0.0))[0:1])
        for c in range(LON):
            own_edge[c, 0:1, :] = first[c : c + 1, :]
            own_edge[c, 1:2, :] = mine[0]
            own_edge[c, 2:3, :] = second[c : c + 1, :]
            own_edge[c, 3:4, :] = mine[1]
        to_row(0, lambda jj: copy_to(own_edge.at[jj], edges.at[j], sem_c.at[0], sem_c.at[1], at_lon(jj)))
        edges[pl.ds(j, 1)] = own_edge[pl.ds(j, 1)]

    fill_halo(0)

    def second(a, r, v):
        xs[1, a, 1 + r, C0 : C0 + COLS, :] = v

    def second_early(a, r, v):
        second(a, r, v)
        nat[1, a, r * COLS : (r + 1) * COLS, :] = to_state(a, r, v)

    sweep(0, second_early)
    start_phase_1(1)

    take_bytes(other_bases, sem_b.at[1])
    for r in range(LAT):
        row_bases[r : r + 1, :] = other_bases[r]
    base = lanes_at(row_bases[...], jnp.where(lane8 < 64, 96 + lane8 % 32, 96 + (LON - 1) * (lane8 % 2)))
    col = fold(jnp.where(at_row, base, 0)) & (LON - 1)
    offset = (lane8 & 1) + COLS * ((lane8 // 2) & 1)
    anchors = []
    for t in range(2):
        a = jnp.zeros((8, 128), I32)
        for v in range(4):
            a = a + jnp.where(col + t == sub8 + 8 * v, row_metas[8 * v : 8 * v + 8, :], 0)
        anchors.append(fold(a))
    side = jnp.where((lane8 + 4) % 8 < 4, 1, 0)
    groups = []
    for at in (lane8 // 4, 32 + lane8 // 4, 64 + 2 * ((lane8 + 4) // 8) + side):
        g = [lanes_at(col, at)] + [(lanes_at(a, at) + offset) & 127 for a in anchors]
        groups.append([jnp.concatenate([v, v], axis=0) for v in g])

    own_row = lanes_at(total, 96 + lane8 // 4) >> 5
    packed_row = jnp.where(lane8 < 64, pltpu.roll(own_row, 8 * i, 1), pltpu.roll(own_row, 8 * i + 64, 1))
    rows_full = jnp.concatenate([own_row, own_row], axis=0)
    rows_packed = jnp.concatenate([packed_row, packed_row], axis=0)

    def phase_2(n):
        picked = []
        for g in range(3):
            at_col, first, second = groups[g]
            for t in range(2):
                index = second if t else first
                acc = jnp.zeros((PIECE, 128), F32)
                for c in range(LON):
                    acc = jnp.where(at_col == c - t, lanes_at(r1[n, c], index), acc)
                picked.append(acc)
            if g < 2:
                for t in range(2):
                    xb[n, g, t] = picked[2 * g + t]
                copy_to(
                    xb.at[n, g], xr.at[n, i], sem_2.at[n, 0], sem_2.at[n, 1], across((LAT - 1) * g)
                )
        xbi[n] = jnp.where(lane16 < 64, picked[4], pltpu.roll(picked[5], 64, 1))

        def send_inner(o, c):
            copy_to(xbi.at[n], xr.at[n, i, 0], sem_2.at[n, 2], sem_2.at[n, 1], across(o))
            return c

        lax.fori_loop(1, LAT - 1, send_inner, 0)

    def pick_rows(n):
        @pl.when(lat_edge)
        def _():
            take_bytes(xr.at[n], sem_2.at[n, 1])
            for s in range(2):
                for t in range(2):
                    acc = jnp.zeros((PIECE, 128), F32)
                    for r in range(LAT):
                        acc = jnp.where(rows_full + s == r, xr[n, r, t], acc)
                    ys[n, s, t] = acc

        @pl.when(jnp.logical_not(lat_edge))
        def _():
            take_bytes(xr.at[n, :, 0], sem_2.at[n, 1])
            for s in range(2):
                acc = jnp.zeros((PIECE, 128), F32)
                for r in range(LAT):
                    acc = jnp.where(rows_packed + s == r, xr[n, r, 0], acc)
                ys[n, s, 0] = pltpu.roll(acc, lax.rem(128 - 8 * i, 128), 1)
                ys[n, s, 1] = pltpu.roll(acc, 64 - 8 * i, 1)

    def phase_3(n):
        z = jnp.concatenate([ys[n, 0, 0], ys[n, 1, 0], ys[n, 0, 1], ys[n, 1, 1]], axis=0)
        z = jnp.concatenate([z, z], axis=0).T
        for jj in range(LON):
            zb[n, jj] = z[4 * jj : 4 * jj + 4, :]

        def send(jj):
            copy_to(zb.at[n, jj], dd.at[n, j], sem_3.at[n, 0], sem_3.at[n, 1], at_lon(jj))

        @pl.when(lat_edge)
        def _():
            to_row(0, send)

        @pl.when(jnp.logical_not(lat_edge))
        def _():
            @pl.when(j != 0)
            def _():
                send(0)

            @pl.when(j != LON - 1)
            def _():
                send(LON - 1)

    def ghost_columns(n):
        dd[n, pl.ds(j, 1)] = zb[n, pl.ds(j, 1)]
        take_bytes(dd.at[n, pl.ds(0, LON - 1)], sem_3.at[n, 1])
        lane32 = iota((LON, 128), 1)
        for h in range(2):
            both = jnp.where(lane32 < 64, dd[n, :, 2 * h, :], pltpu.roll(dd[n, :, 2 * h + 1, :], 64, 1))
            turned[128 * h : 128 * (h + 1), :] = jnp.concatenate([both] * 4, axis=0).T
        g = []
        for a in range(4):
            cells_at = jnp.zeros((16, 128), F32)
            for d in range(4):
                v = turned[pl.ds(4 * a + d, 16, stride=16), :]
                cells_at = jnp.where(lane16 // LON == d, v, cells_at)
            g.append(
                lax.dot_general(
                    mix, cells_at, (((1,), (0,)), ((), ())),
                    precision=lax.Precision.HIGHEST, preferred_element_type=F32,
                )
            )
        ghost[0] = cosine * g[0] - sine * g[1]
        ghost[1] = sine * g[0] + cosine * g[1]
        ghost[2] = g[2]
        ghost[3] = g[3]
        for side, edge, r_in, r_out in SIDES_LAT:
            @pl.when(i == edge)
            def _():
                for a in range(4):
                    v = ghost[a, side * COLS : (side + 1) * COLS, :]
                    v = v * root[0, r_in] if a == 3 else v / root[1, r_in]
                    xs[n, a, r_out, C0 : C0 + COLS, :] = v

        for side, edge, c_in, c_out in SIDES_LON:
            @pl.when(j == edge)
            def _():
                at = 2 * COLS + side * ROWS
                for a in range(4):
                    for r in range(ROWS):
                        v = ghost[a, at + r : at + r + 1, :]
                        if a == 3:
                            v = v * root[0, r, c_in : c_in + 1, :]
                        else:
                            v = v / root[1, r, c_in : c_in + 1, :]
                        xs[n, a, 1 + r, c_out : c_out + 1, :] = v

    take_bytes(r1.at[0, pl.ds(0, LON - 1)], sem_1.at[0, 1])
    phase_2(0)

    @pl.when(lat_edge)
    def _():
        take_bytes(edges.at[pl.ds(0, LON - 1)], sem_c.at[1])
        for f in range(2):
            for c in range(LON):
                row_edges[f, c : c + 1, :] = edges[c, f : f + 1, :]
        here = lane8 // COLS == sub8
        for b in range(4):
            def row(f, start):
                v = lanes_at(row_edges[f, 8 * b : 8 * b + 8, :], start + lane8 % COLS)
                return fold(jnp.where(here, v, 0.0))

            rows = [row(1, COLS * f) for f in range(7)]
            for k in range(4):
                for t in range(2):
                    for s in range(2):
                        m = 4 * (4 * k + 2 * t + s) + b
                        wv[m : m + 1, :] = jnp.where(rows[6] == t + 2.0 * s, rows[k], 0.0)[0:1]
            wv[64 + b : 65 + b, :] = rows[4][0:1]
            wv[68 + b : 69 + b, :] = rows[5][0:1]
            for f in range(2):
                v = jnp.zeros((8, 128), F32)
                for d in range(4):
                    v = jnp.where(sub8 % 4 == d, row(0, LON * d + COLS * f), v)
                cv[f, b] = v

    @pl.when(jnp.logical_not(lat_edge))
    def _():
        @pl.when(lon_edge)
        def _():
            take_bytes(edges.at[0], sem_c.at[1])

        @pl.when(jnp.logical_not(lon_edge))
        def _():
            take_bytes(edges.at[pl.ds(0, 2)], sem_c.at[1])

    for side, c in ((0, 0), (1, LON - 1)):
        own_lane = lane8 % COLS == (COLS - 1) * side
        coefs = jnp.broadcast_to(edges[c, 2:3, :], (8, 128))
        infos = jnp.broadcast_to(edges[c, 3:4, :], (8, 128))
        rows = [jnp.where(own_lane, lanes_at(infos, COLS * f + lane8 // COLS), 0.0) for f in range(7)]
        for k in range(4):
            for t in range(2):
                for s in range(2):
                    m = 4 * k + 2 * t + s
                    ww[side, m : m + 1, :] = jnp.where(rows[6] == t + 2.0 * s, rows[k], 0.0)[0:1]
        ww[side, 16:17, :] = rows[4][0:1]
        ww[side, 17:18, :] = rows[5][0:1]
        for f in range(2):
            cw[side, f] = lanes_at(coefs, LON * (sub8 % 4) + ROWS * f + lane8 // COLS)

    own_lanes = [lane8 % COLS == (COLS - 1) * side for side in range(2)]

    def swap(v):
        return pltpu.roll(v, 4, 0)

    def rotated(g, cos, sin):
        return cos * g + jnp.where(low8, -sin, sin) * swap(g)

    pick_rows(0)
    take_bytes(r1.at[1, pl.ds(0, LON - 1)], sem_1.at[1, 1])

    @pl.when(lat_edge)
    def _():
        sign = jnp.where(i == 0, 1.0, -1.0)
        start = jnp.where(i == 0, 0, 128 - COLS)
        here = jnp.logical_and(lane8 >= start, lane8 < start + COLS)
        for b in range(4):
            index = 4 * (8 * b + lane16 // COLS)
            g = jnp.zeros((PIECE, 128), F32)
            for k in range(4):
                for t in range(2):
                    for s in range(2):
                        m = 4 * (4 * k + 2 * t + s) + b
                        g = g + lanes_at(ys[0, s, t], index + k) * wv[m : m + 1, :]
            u = rotated(g[0:8], wv[64 + b : 65 + b, :], wv[68 + b : 69 + b, :])
            w = g[8:16]
            fc, bc = cv[0, b], cv[1, b]
            d0 = fc * u + jnp.where(low8, sign * bc * swap(w), 0.0)
            d1 = jnp.where(low8, fc * w, (sign * THIRD) * swap(u))
            for o in range(8):
                c = 8 * b + o
                shift = lax.rem(start + 128 - COLS * o, 128)
                r1[1, c, 0:8, :] = r1[1, c, 0:8, :] + jnp.where(here, pltpu.roll(d0, shift, 1), 0.0)
                r1[1, c, 8:16, :] = r1[1, c, 8:16, :] + jnp.where(here, pltpu.roll(d1, shift, 1), 0.0)

    for side, c in ((0, 0), (1, LON - 1)):
        sign = 1.0 - 2.0 * side
        g = jnp.zeros((PIECE, 128), F32)
        for k in range(4):
            for t in range(2):
                for s in range(2):
                    m = 4 * k + 2 * t + s
                    g = g + ys[0, s, t, :, 4 * c + k : 4 * c + k + 1] * ww[side, m : m + 1, :]
        u = rotated(g[0:8], ww[side, 16:17, :], ww[side, 17:18, :])
        w = g[8:16]
        fc, bc = cw[side, 0], cw[side, 1]
        d0 = fc * u + jnp.where(low8, 0.0, sign * bc * w)
        d1 = jnp.where(low8, fc * w, (sign * THIRD) * u)
        r1[1, c, 0:8, :] = r1[1, c, 0:8, :] + jnp.where(own_lanes[side], d0, 0.0)
        r1[1, c, 8:16, :] = r1[1, c, 8:16, :] + jnp.where(own_lanes[side], d1, 0.0)

    phase_2(1)

    phase_3(0)

    @pl.when(is_edge)
    def _():
        ghost_columns(0)
        sweep(0, second)

    start_halo(1)
    pick_rows(1)
    phase_3(1)
    fill_halo(1)

    @pl.when(is_edge)
    def _():
        ghost_columns(1)

    def third(a, r, v):
        out[a, r] = to_state(a, r, v)

    sweep(1, third)

    take_bytes(hv_row, sem_hv.at[0])
    take_bytes(hv_col, sem_hv.at[3])
    take_bytes(metas.at[pl.ds(0, LON - 1)], sem_m.at[0])
    take_bytes(other_bases, sem_b.at[0])

    @pl.when(is_edge)
    def _():
        take_bytes(edges.at[pl.ds(0, LON - 1)], sem_c.at[0])

    for n in range(2):
        take_bytes(h_row.at[n], sem_h.at[n, 0])
        take_bytes(h_col.at[n], sem_h.at[n, 3])
        take_bytes(r1.at[n, pl.ds(0, LON - 1)], sem_1.at[n, 0])
        take_bytes(xb.at[n], sem_2.at[n, 0])
        take_bytes(r1.at[n, pl.ds(0, LAT - 2)], sem_2.at[n, 2])

        @pl.when(lat_edge)
        def _():
            take_bytes(dd.at[n, pl.ds(0, LON - 1)], sem_3.at[n, 0])

        @pl.when(jnp.logical_not(lat_edge))
        def _():
            @pl.when(lon_edge)
            def _():
                take_bytes(dd.at[n, 0], sem_3.at[n, 0])

            @pl.when(jnp.logical_not(lon_edge))
            def _():
                take_bytes(dd.at[n, pl.ds(0, 2)], sem_3.at[n, 0])


def body(viscosity, forcing, send_cell, partner, ghost_src, ghost_weight, ghost_angle):
    dma = pltpu.SemaphoreType.DMA

    def floats(*shape):
        return pltpu.VMEM(shape, F32)

    def ints(*shape):
        return pltpu.VMEM(shape, I32)

    scratch = [
        floats(ROWS, COLS, DEPTH),
        floats(4, ROWS, COLS, DEPTH),
        ints(8, 128),
        ints(1, 4),
        ints(1, GHOSTS),
        floats(1, GHOSTS),
        floats(4, GHOSTS),
        floats(ROWS + 2, C0 + COLS + 8, DEPTH),
        floats(2, COLS, DEPTH),
        floats(2, ROWS, DEPTH),
        floats(2, COLS, DEPTH),
        floats(2, ROWS, DEPTH),
        floats(2, 4, ROWS + 2, C0 + COLS + 8, DEPTH),
        floats(6, ROWS, COLS, DEPTH),
        floats(ROWS, COLS, DEPTH),
        floats(4, ROWS, COLS, DEPTH),
        floats(3, ROWS, COLS, DEPTH),
        floats(2, 2, 4, COLS, DEPTH),
        floats(2, 2, 4, ROWS, DEPTH),
        floats(2, 2, 4, COLS, DEPTH),
        floats(2, 2, 4, ROWS, DEPTH),
        ints(1, 128),
        ints(LON, 1, 128),
        ints(LON, 128),
        ints(1, 128),
        ints(LAT, 1, 128),
        ints(LAT, 128),
        floats(8, 128),
        floats(128, 128),
        floats(2, 4, CELLS, DEPTH),
        floats(2, LON * PIECE, CELLS),
        floats(2, LON, PIECE, CELLS),
        floats(LON, 4, 128),
        floats(LON, 4, 128),
        floats(2, LON, 128),
        floats(2, 2, 2, PIECE, 128),
        floats(2, PIECE, 128),
        floats(2, LAT, 2, PIECE, 128),
        floats(2, 2, 2, PIECE, 128),
        floats(2, LON, 4, 128),
        floats(2, LON, 4, 128),
        floats(256, 128),
        floats(4, GHOSTS, DEPTH),
        floats(72, 128),
        floats(2, 24, 128),
        floats(2, 4, 8, 128),
        floats(2, 2, 8, 128),
        dma((7,)), dma((4,)), dma((2,)), dma((2,)), dma((2, 4)), dma((2, 2)), dma((2,)),
        dma((2, 3)), dma((2, 2)),
    ]
    state = pl.pallas_call(
        kernel,
        out_shape=jax.ShapeDtypeStruct((4, ROWS, COLS, DEPTH), F32),
        in_specs=[pl.BlockSpec(memory_space=pl.ANY)] * 7,
        out_specs=pl.BlockSpec(memory_space=pltpu.VMEM),
        scratch_shapes=scratch,
        compiler_params=pltpu.CompilerParams(
            collective_id=0, has_side_effects=True, vmem_limit_bytes=63 << 20
        ),
    )(
        viscosity.reshape(ROWS, COLS, DEPTH),
        forcing.reshape(4, ROWS, COLS, DEPTH),
        send_cell.reshape(LAT, 4 * LON),
        partner.reshape(1, 4),
        ghost_src.reshape(1, GHOSTS),
        ghost_angle.reshape(1, GHOSTS),
        jnp.swapaxes(ghost_weight, 3, 4).reshape(4, GHOSTS),
    )
    return state[:, None]


def solution(mesh):
    placed = (
        P("panel", "lat", "lon", None),
        P(None, "panel", "lat", "lon", None),
        P("panel", "lat", "lon", None),
        P("panel", "lat", "lon", None),
        P("panel", "lat", "lon", None),
        P("panel", "lat", "lon", None, None),
        P("panel", "lat", "lon", None),
    )
    return jax.shard_map(
        body,
        mesh=mesh,
        in_specs=placed,
        out_specs=P(None, "panel", "lat", "lon", None),
        check_vma=False,
    )
```

```python
import math

import jax
import jax.numpy as jnp
from jax import lax
from jax.experimental import pallas as pl
from jax.experimental.pallas import tpu as pltpu
from jax.sharding import PartitionSpec as P

MESH = pl.DeviceIdType.MESH
LAT, LON = 8, 32
ROWS, COLS, DEPTH = 8, 16, 128
CELLS = ROWS * COLS
GHOSTS = 48
PIECE = 4 * DEPTH // LON
C0 = 8
F32, I32 = jnp.float32, jnp.int32
SIX = math.sqrt(6.0)
THIRD = 0.25 / SIX


def copy_to(src, dst, send, recv, device):
    pltpu.make_async_remote_copy(
        src_ref=src,
        dst_ref=dst,
        send_sem=send,
        recv_sem=recv,
        device_id=device,
        device_id_type=MESH,
    ).start()


def take_bytes(ref, sem):
    pltpu.make_async_copy(ref, ref, sem).wait()


def iota(shape, dim):
    return lax.broadcasted_iota(I32, shape, dim)


def kernel(
    visc_in, rhs_in, cells_in, partner_in, src_in, angle_in, weight_in, out,
    visc, rhs, cells, partner, src, angle, weight,
    pv, hv_row, hv_col, hv_srow, hv_scol,
    xs, face, coef, force, root,
    h_srow, h_scol, h_row, h_col,
    meta, metas, row_metas, bases, other_bases, row_bases, info, square,
    nat, tb, r1, own_edge, edges, row_edges, xb, xbi, xr, ys, zb, dd, turned, ghost, wv, ww, cv, cw,
    sem_in, sem_hv, sem_m, sem_b, sem_h, sem_1, sem_c, sem_2, sem_3, ready,
):
    p = lax.axis_index("panel")
    i = lax.axis_index("lat")
    j = lax.axis_index("lon")
    q = 1 - p
    lat_edge = jnp.logical_or(i == 0, i == LAT - 1)
    lon_edge = jnp.logical_or(j == 0, j == LON - 1)
    is_edge = jnp.logical_or(lat_edge, lon_edge)

    def at_lon(jj):
        return {"panel": p, "lat": i, "lon": jj}

    def at_lat(ii):
        return {"panel": p, "lat": ii, "lon": j}

    def across(ii):
        return {"panel": q, "lat": ii, "lon": j}

    south, north = lax.rem(i + LAT - 1, LAT), lax.rem(i + 1, LAT)
    west, east = lax.rem(j + LON - 1, LON), lax.rem(j + 1, LON)

    def to_row(n, send):
        def step(o, c):
            send(lax.rem(j + o, LON))
            return c

        lax.fori_loop(1, LON, step, 0)

    barrier = pltpu.get_barrier_semaphore()

    def greet(device):
        pl.semaphore_signal(barrier, 1, device_id=device, device_id_type=MESH)

    def greet_lat(o, c):
        greet(at_lat(lax.rem(i + o, LAT)))
        return c

    greet(across(i))
    lax.fori_loop(1, LAT, greet_lat, 0)
    to_row(0, lambda jj: greet(at_lon(jj)))

    moves = [
        pltpu.make_async_copy(a, b, sem_in.at[n])
        for n, (a, b) in enumerate(
            (
                (visc_in, visc), (cells_in, cells), (partner_in, partner), (weight_in, weight),
                (src_in, src), (angle_in, angle), (rhs_in, rhs),
            )
        )
    ]
    for move in moves:
        move.start()
    for move in moves:
        move.wait()
    sub8 = iota((8, 128), 0)
    lane8 = iota((8, 128), 1)
    lane16 = iota((16, 128), 1)
    low8 = sub8 < 4

    def lanes_at(v, index):
        return jnp.take_along_axis(v, index, axis=1, mode="promise_in_bounds")

    def fold(v):
        for h in (4, 2, 1):
            v = v + pltpu.roll(v, h, 0)
        return v

    receiver_row = jnp.where(lane8 < 32, 0, jnp.where(lane8 < 64, LAT - 1, (lane8 - 64) // 2))
    at_row = sub8 == receiver_row
    asked = lanes_at(cells[...], jnp.where(lane8 < 64, 4 * (lane8 % 32), 124 * (lane8 % 2)))
    asked = fold(jnp.where(at_row, asked, 0))
    my_base = jnp.broadcast_to(partner[0:1, 0:1], (8, 128))
    asked = jnp.where(lane8 < 96, asked, jnp.where(lane8 == 96 + j, my_base, 0))
    meta[...] = asked[0:1]
    metas[pl.ds(j, 1)] = meta[...][None]
    hv_srow[0] = visc[0]
    hv_srow[1] = visc[ROWS - 1]
    for r in range(ROWS):
        hv_scol[0, r : r + 1, :] = visc[r, 0:1, :]
        hv_scol[1, r : r + 1, :] = visc[r, COLS - 1 : COLS, :]
    pv[1 : ROWS + 1, C0 : C0 + COLS, :] = visc[...]

    info[...] = jnp.zeros((8, 128), F32)
    info[0:4, 0:GHOSTS] = weight[...] / jnp.sum(weight[...], axis=0, keepdims=True)
    info[4:5, 0:GHOSTS] = jnp.cos(angle[...])
    info[5:6, 0:GHOSTS] = jnp.sin(angle[...])
    info[6:7, 0:GHOSTS] = src[...].astype(F32)
    square[...] = jnp.zeros((128, 128), F32)
    square[0:8, :] = info[...]
    columns = square[...].T[0:GHOSTS]

    def column(k):
        return jnp.broadcast_to(columns[:, k : k + 1], (GHOSTS, 128))

    cosine = column(4)
    sine = column(5)
    lane48 = iota((GHOSTS, 128), 1)
    mix = jnp.zeros((GHOSTS, 128), F32)
    for k in range(4):
        mix = mix + jnp.where(lane48 // 4 == k, column(k), 0.0)
    which = (lane48 // 2 % 2 + 2 * (lane48 % 2)).astype(F32)
    mix = jnp.where(which == column(6), mix, 0.0)[:, 0:16]

    pl.semaphore_wait(barrier, LAT + LON - 1)
    pl.semaphore_signal(ready, 1, device_id=across(i), device_id_type=MESH)

    copy_to(hv_srow.at[0], hv_row.at[1], sem_hv.at[0], sem_hv.at[1], at_lat(south))
    copy_to(hv_srow.at[1], hv_row.at[0], sem_hv.at[0], sem_hv.at[1], at_lat(north))
    copy_to(hv_scol.at[0], hv_col.at[1], sem_hv.at[3], sem_hv.at[2], at_lon(west))
    copy_to(hv_scol.at[1], hv_col.at[0], sem_hv.at[3], sem_hv.at[2], at_lon(east))
    to_row(0, lambda jj: copy_to(meta, metas.at[j], sem_m.at[0], sem_m.at[1], at_lon(jj)))

    take_bytes(hv_row, sem_hv.at[1])
    take_bytes(hv_col, sem_hv.at[2])
    pv[0, C0 : C0 + COLS, :] = jnp.where(i == 0, visc[0], hv_row[0])
    pv[ROWS + 1, C0 : C0 + COLS, :] = jnp.where(i == LAT - 1, visc[ROWS - 1], hv_row[1])
    first = jnp.where(j == 0, hv_scol[0], hv_col[0])
    last = jnp.where(j == LON - 1, hv_scol[1], hv_col[1])
    for r in range(ROWS):
        pv[1 + r, C0 - 1 : C0, :] = first[r : r + 1, :]
        pv[1 + r, C0 + COLS : C0 + COLS + 1, :] = last[r : r + 1, :]

    def ahead(v):
        return pltpu.roll(v, DEPTH - 1, 1)

    def behind(v):
        return pltpu.roll(v, 1, 1)

    top, bottom = lane16 == DEPTH - 1, lane16 == 0

    for r in range(ROWS):
        e = pv[1 + r, C0 : C0 + COLS, :]
        near = (
            pv[r, C0 : C0 + COLS, :],
            pv[2 + r, C0 : C0 + COLS, :],
            pv[1 + r, C0 - 1 : C0 - 1 + COLS, :],
            pv[1 + r, C0 + 1 : C0 + 1 + COLS, :],
            jnp.where(bottom, e, behind(e)),
            jnp.where(top, e, ahead(e)),
        )
        dsum = jnp.zeros_like(e)
        for k, o in enumerate(near):
            f = 2.0 * e * o / (e + o)
            face[k, r] = f
            dsum = dsum + f
        half = 0.5 / dsum
        coef[r] = half
        se = jnp.sqrt(e)
        six = SIX * se
        root[0, r] = se
        root[1, r] = six
        root[2, r] = 1.0 / se
        at = slice(r * COLS, (r + 1) * COLS)
        for a in range(3):
            w = rhs[a, r] * six
            force[a, r] = w
            x = half * w
            xs[0, a, 1 + r, C0 : C0 + COLS, :] = x
            nat[0, a, at, :] = x * six
        w = -0.5 * (rhs[3, r] * se)
        force[3, r] = w
        xs[0, 3, 1 + r, C0 : C0 + COLS, :] = w
        nat[0, 3, at, :] = -0.5 * rhs[3, r]

    def sweep(n, out_at):
        for r in range(ROWS):
            def get(a, dr, dc):
                return xs[n, a, 1 + r + dr, C0 + dc : C0 + dc + COLS, :]

            e = pv[1 + r, C0 : C0 + COLS, :]
            half = coef[r]
            around = []
            for a in range(4):
                v = get(a, 0, 0)
                around.append(
                    (
                        get(a, -1, 0),
                        get(a, 1, 0),
                        get(a, 0, -1),
                        get(a, 0, 1),
                        jnp.where(bottom, 0.0, behind(v)),
                        jnp.where(top, 0.0, ahead(v)),
                        v,
                    )
                )
            pr = around[3]
            div = jnp.zeros_like(e)
            for a in range(3):
                total = force[a, r] - 0.5 * (pr[2 * a + 1] - pr[2 * a])
                for k in range(6):
                    total = total + face[k, r] * around[a][k]
                x = 0.5 * around[a][6] + half * total
                out_at(a, r, x)
                div = div + (around[a][2 * a + 1] - around[a][2 * a])
            out_at(3, r, 0.5 * pr[6] + force[3, r] - 0.25 * (e * div))

    def to_state(a, r, v):
        return v * (root[2, r] if a == 3 else root[1, r])

    def pack(n, field, where):
        t = nat[n, field].T
        for w in where:
            for d in range(4):
                tb[n, pl.ds(4 * w + d, LON, stride=PIECE), :] = t[LON * d : LON * (d + 1), :]

    def piece(n, jj):
        return tb.at[n, pl.ds(pl.multiple_of(jj * PIECE, PIECE), PIECE)]

    def pack_all(n):
        for a in range(4):
            pack(n, a, (a,))

    def start_phase_1(n):
        to_row(
            0,
            lambda jj: copy_to(piece(n, jj), r1.at[n, j], sem_1.at[n, 0], sem_1.at[n, 1], at_lon(jj)),
        )
        r1[n, pl.ds(j, 1)] = tb[n, pl.ds(pl.multiple_of(j * PIECE, PIECE), PIECE), :][None]

    def start_halo(n):
        for a in range(4):
            h_srow[n, 0, a] = xs[n, a, 1, C0 : C0 + COLS, :]
            h_srow[n, 1, a] = xs[n, a, ROWS, C0 : C0 + COLS, :]
            for r in range(ROWS):
                h_scol[n, 0, a, r : r + 1, :] = xs[n, a, 1 + r, C0 : C0 + 1, :]
                h_scol[n, 1, a, r : r + 1, :] = xs[n, a, 1 + r, C0 + COLS - 1 : C0 + COLS, :]
        copy_to(h_srow.at[n, 0], h_row.at[n, 1], sem_h.at[n, 0], sem_h.at[n, 1], at_lat(south))
        copy_to(h_srow.at[n, 1], h_row.at[n, 0], sem_h.at[n, 0], sem_h.at[n, 1], at_lat(north))
        copy_to(h_scol.at[n, 0], h_col.at[n, 1], sem_h.at[n, 3], sem_h.at[n, 2], at_lon(west))
        copy_to(h_scol.at[n, 1], h_col.at[n, 0], sem_h.at[n, 3], sem_h.at[n, 2], at_lon(east))

    SIDES_LAT = ((0, 0, 0, 0), (1, LAT - 1, ROWS - 1, ROWS + 1))
    SIDES_LON = ((0, 0, 0, C0 - 1), (1, LON - 1, COLS - 1, C0 + COLS))

    def fill_halo(n):
        take_bytes(h_row.at[n], sem_h.at[n, 1])
        take_bytes(h_col.at[n], sem_h.at[n, 2])
        for side, edge, r_in, r_out in SIDES_LAT:
            for a in range(4):
                xs[n, a, r_out, C0 : C0 + COLS, :] = jnp.where(i == edge, 0.0, h_row[n, side, a])
        for side, edge, c_in, c_out in SIDES_LON:
            for a in range(4):
                v = jnp.where(j == edge, 0.0, h_col[n, side, a])
                for r in range(ROWS):
                    xs[n, a, 1 + r, c_out : c_out + 1, :] = v[r : r + 1, :]

    start_halo(0)
    pack_all(0)
    start_phase_1(0)

    fill_halo(0)

    def second(a, r, v):
        xs[1, a, 1 + r, C0 : C0 + COLS, :] = v

    def second_early(a, r, v):
        second(a, r, v)
        nat[1, a, r * COLS : (r + 1) * COLS, :] = to_state(a, r, v)

    sweep(0, second_early)
    pack_all(1)
    start_phase_1(1)

    take_bytes(metas.at[pl.ds(0, LON - 1)], sem_m.at[1])
    for c in range(LON):
        row_metas[c : c + 1, :] = metas[c]
    total = row_metas[0:8] + row_metas[8:16] + row_metas[16:24] + row_metas[24:32]
    total = jnp.where(lane8 < 96, 0, fold(total))
    bases[...] = total[0:1]

    def send_bases(o, c):
        copy_to(bases, other_bases.at[i], sem_b.at[0], sem_b.at[1], across(o))
        return c

    pl.semaphore_wait(ready, 1)
    lax.fori_loop(0, LAT, send_bases, 0)

    @pl.when(is_edge)
    def _():
        def pressure(r):
            return (0.5 * SIX) * (pv[1 + r, C0 : C0 + COLS, :] * coef[r])

        low = i == 0
        square[...] = jnp.zeros((128, 128), F32)
        square[0:COLS, :] = jnp.where(low, coef[0] * face[0, 0], coef[ROWS - 1] * face[1, ROWS - 1])
        square[COLS : 2 * COLS, :] = jnp.where(low, pressure(0), pressure(ROWS - 1))
        for r in range(ROWS):
            at = 2 * COLS + r
            f = jnp.where(
                j == 0,
                coef[r, 0:1, :] * face[2, r, 0:1, :],
                coef[r, COLS - 1 : COLS, :] * face[3, r, COLS - 1 : COLS, :],
            )
            b = pressure(r)
            square[at : at + 1, :] = f
            square[at + ROWS : at + ROWS + 1, :] = jnp.where(j == 0, b[0:1], b[COLS - 1 : COLS])
        turn = square[...].T
        lane32 = iota((LON, 128), 1)
        first = jnp.zeros((LON, 128), F32)
        second = jnp.zeros((LON, 128), F32)
        for d in range(4):
            slab = turn[LON * d : LON * (d + 1), :]
            v = pltpu.roll(slab, LON * d, 1) if d else slab
            first = jnp.where(lane32 // LON == d, v, first)
            second = jnp.where(lane32 // LON == d, pltpu.roll(slab, (LON * d + 96) % 128, 1), second)
        mine = []
        for at in (jnp.where(low, 0, COLS), 2 * COLS + jnp.where(j == 0, 0, ROWS)):
            v = lanes_at(info[...], at + lane8 % COLS)
            mine.append(fold(jnp.where(lane8 // COLS == sub8, v, 0.0))[0:1])
        for c in range(LON):
            own_edge[c, 0:1, :] = first[c : c + 1, :]
            own_edge[c, 1:2, :] = mine[0]
            own_edge[c, 2:3, :] = second[c : c + 1, :]
            own_edge[c, 3:4, :] = mine[1]
        to_row(0, lambda jj: copy_to(own_edge.at[jj], edges.at[j], sem_c.at[0], sem_c.at[1], at_lon(jj)))
        edges[pl.ds(j, 1)] = own_edge[pl.ds(j, 1)]

    take_bytes(other_bases, sem_b.at[1])
    for r in range(LAT):
        row_bases[r : r + 1, :] = other_bases[r]
    base = lanes_at(row_bases[...], jnp.where(lane8 < 64, 96 + lane8 % 32, 96 + (LON - 1) * (lane8 % 2)))
    col = fold(jnp.where(at_row, base, 0)) & (LON - 1)
    offset = (lane8 & 1) + COLS * ((lane8 // 2) & 1)
    anchors = []
    for t in range(2):
        a = jnp.zeros((8, 128), I32)
        for v in range(4):
            a = a + jnp.where(col + t == sub8 + 8 * v, row_metas[8 * v : 8 * v + 8, :], 0)
        anchors.append(fold(a))
    side = jnp.where((lane8 + 4) % 8 < 4, 1, 0)
    groups = []
    for at in (lane8 // 4, 32 + lane8 // 4, 64 + 2 * ((lane8 + 4) // 8) + side):
        g = [lanes_at(col, at)] + [(lanes_at(a, at) + offset) & 127 for a in anchors]
        groups.append([jnp.concatenate([v, v], axis=0) for v in g])

    own_row = lanes_at(total, 96 + lane8 // 4) >> 5
    packed_row = jnp.where(lane8 < 64, pltpu.roll(own_row, 8 * i, 1), pltpu.roll(own_row, 8 * i + 64, 1))
    rows_full = jnp.concatenate([own_row, own_row], axis=0)
    rows_packed = jnp.concatenate([packed_row, packed_row], axis=0)

    def phase_2(n):
        picked = []
        for g in range(3):
            at_col, first, second = groups[g]
            for t in range(2):
                index = second if t else first
                acc = jnp.zeros((PIECE, 128), F32)
                for c in range(LON):
                    acc = jnp.where(at_col == c - t, lanes_at(r1[n, c], index), acc)
                picked.append(acc)
            if g < 2:
                for t in range(2):
                    xb[n, g, t] = picked[2 * g + t]
                copy_to(
                    xb.at[n, g], xr.at[n, i], sem_2.at[n, 0], sem_2.at[n, 1], across((LAT - 1) * g)
                )
        xbi[n] = jnp.where(lane16 < 64, picked[4], pltpu.roll(picked[5], 64, 1))

        def send_inner(o, c):
            copy_to(xbi.at[n], xr.at[n, i, 0], sem_2.at[n, 2], sem_2.at[n, 1], across(o))
            return c

        lax.fori_loop(1, LAT - 1, send_inner, 0)

    def pick_rows(n):
        @pl.when(lat_edge)
        def _():
            take_bytes(xr.at[n], sem_2.at[n, 1])
            for s in range(2):
                for t in range(2):
                    acc = jnp.zeros((PIECE, 128), F32)
                    for r in range(LAT):
                        acc = jnp.where(rows_full + s == r, xr[n, r, t], acc)
                    ys[n, s, t] = acc

        @pl.when(jnp.logical_not(lat_edge))
        def _():
            take_bytes(xr.at[n, :, 0], sem_2.at[n, 1])
            for s in range(2):
                acc = jnp.zeros((PIECE, 128), F32)
                for r in range(LAT):
                    acc = jnp.where(rows_packed + s == r, xr[n, r, 0], acc)
                ys[n, s, 0] = pltpu.roll(acc, lax.rem(128 - 8 * i, 128), 1)
                ys[n, s, 1] = pltpu.roll(acc, 64 - 8 * i, 1)

    def phase_3(n):
        z = jnp.concatenate([ys[n, 0, 0], ys[n, 1, 0], ys[n, 0, 1], ys[n, 1, 1]], axis=0)
        z = jnp.concatenate([z, z], axis=0).T
        for jj in range(LON):
            zb[n, jj] = z[4 * jj : 4 * jj + 4, :]

        def send(jj):
            copy_to(zb.at[n, jj], dd.at[n, j], sem_3.at[n, 0], sem_3.at[n, 1], at_lon(jj))

        @pl.when(lat_edge)
        def _():
            to_row(0, send)

        @pl.when(jnp.logical_not(lat_edge))
        def _():
            @pl.when(j != 0)
            def _():
                send(0)

            @pl.when(j != LON - 1)
            def _():
                send(LON - 1)

    def ghost_columns(n):
        dd[n, pl.ds(j, 1)] = zb[n, pl.ds(j, 1)]
        take_bytes(dd.at[n, pl.ds(0, LON - 1)], sem_3.at[n, 1])
        lane32 = iota((LON, 128), 1)
        for h in range(2):
            both = jnp.where(lane32 < 64, dd[n, :, 2 * h, :], pltpu.roll(dd[n, :, 2 * h + 1, :], 64, 1))
            turned[128 * h : 128 * (h + 1), :] = jnp.concatenate([both] * 4, axis=0).T
        g = []
        for a in range(4):
            cells_at = jnp.zeros((16, 128), F32)
            for d in range(4):
                v = turned[pl.ds(4 * a + d, 16, stride=16), :]
                cells_at = jnp.where(lane16 // LON == d, v, cells_at)
            g.append(
                lax.dot_general(
                    mix, cells_at, (((1,), (0,)), ((), ())),
                    precision=lax.Precision.HIGHEST, preferred_element_type=F32,
                )
            )
        ghost[0] = cosine * g[0] - sine * g[1]
        ghost[1] = sine * g[0] + cosine * g[1]
        ghost[2] = g[2]
        ghost[3] = g[3]
        for side, edge, r_in, r_out in SIDES_LAT:
            @pl.when(i == edge)
            def _():
                for a in range(4):
                    v = ghost[a, side * COLS : (side + 1) * COLS, :]
                    v = v * root[0, r_in] if a == 3 else v / root[1, r_in]
                    xs[n, a, r_out, C0 : C0 + COLS, :] = v

        for side, edge, c_in, c_out in SIDES_LON:
            @pl.when(j == edge)
            def _():
                at = 2 * COLS + side * ROWS
                for a in range(4):
                    for r in range(ROWS):
                        v = ghost[a, at + r : at + r + 1, :]
                        if a == 3:
                            v = v * root[0, r, c_in : c_in + 1, :]
                        else:
                            v = v / root[1, r, c_in : c_in + 1, :]
                        xs[n, a, 1 + r, c_out : c_out + 1, :] = v

    take_bytes(r1.at[0, pl.ds(0, LON - 1)], sem_1.at[0, 1])
    phase_2(0)

    @pl.when(lat_edge)
    def _():
        take_bytes(edges.at[pl.ds(0, LON - 1)], sem_c.at[1])
        for f in range(2):
            for c in range(LON):
                row_edges[f, c : c + 1, :] = edges[c, f : f + 1, :]
        here = lane8 // COLS == sub8
        for b in range(4):
            def row(f, start):
                v = lanes_at(row_edges[f, 8 * b : 8 * b + 8, :], start + lane8 % COLS)
                return fold(jnp.where(here, v, 0.0))

            rows = [row(1, COLS * f) for f in range(7)]
            for k in range(4):
                for t in range(2):
                    for s in range(2):
                        m = 4 * (4 * k + 2 * t + s) + b
                        wv[m : m + 1, :] = jnp.where(rows[6] == t + 2.0 * s, rows[k], 0.0)[0:1]
            wv[64 + b : 65 + b, :] = rows[4][0:1]
            wv[68 + b : 69 + b, :] = rows[5][0:1]
            for f in range(2):
                v = jnp.zeros((8, 128), F32)
                for d in range(4):
                    v = jnp.where(sub8 % 4 == d, row(0, LON * d + COLS * f), v)
                cv[f, b] = v

    @pl.when(jnp.logical_not(lat_edge))
    def _():
        @pl.when(lon_edge)
        def _():
            take_bytes(edges.at[0], sem_c.at[1])

        @pl.when(jnp.logical_not(lon_edge))
        def _():
            take_bytes(edges.at[pl.ds(0, 2)], sem_c.at[1])

    for side, c in ((0, 0), (1, LON - 1)):
        own_lane = lane8 % COLS == (COLS - 1) * side
        coefs = jnp.broadcast_to(edges[c, 2:3, :], (8, 128))
        infos = jnp.broadcast_to(edges[c, 3:4, :], (8, 128))
        rows = [jnp.where(own_lane, lanes_at(infos, COLS * f + lane8 // COLS), 0.0) for f in range(7)]
        for k in range(4):
            for t in range(2):
                for s in range(2):
                    m = 4 * k + 2 * t + s
                    ww[side, m : m + 1, :] = jnp.where(rows[6] == t + 2.0 * s, rows[k], 0.0)[0:1]
        ww[side, 16:17, :] = rows[4][0:1]
        ww[side, 17:18, :] = rows[5][0:1]
        for f in range(2):
            cw[side, f] = lanes_at(coefs, LON * (sub8 % 4) + ROWS * f + lane8 // COLS)

    own_lanes = [lane8 % COLS == (COLS - 1) * side for side in range(2)]

    def swap(v):
        return pltpu.roll(v, 4, 0)

    def rotated(g, cos, sin):
        return cos * g + jnp.where(low8, -sin, sin) * swap(g)

    pick_rows(0)
    take_bytes(r1.at[1, pl.ds(0, LON - 1)], sem_1.at[1, 1])

    @pl.when(lat_edge)
    def _():
        sign = jnp.where(i == 0, 1.0, -1.0)
        start = jnp.where(i == 0, 0, 128 - COLS)
        here = jnp.logical_and(lane8 >= start, lane8 < start + COLS)
        for b in range(4):
            index = 4 * (8 * b + lane16 // COLS)
            g = jnp.zeros((PIECE, 128), F32)
            for k in range(4):
                for t in range(2):
                    for s in range(2):
                        m = 4 * (4 * k + 2 * t + s) + b
                        g = g + lanes_at(ys[0, s, t], index + k) * wv[m : m + 1, :]
            u = rotated(g[0:8], wv[64 + b : 65 + b, :], wv[68 + b : 69 + b, :])
            w = g[8:16]
            fc, bc = cv[0, b], cv[1, b]
            d0 = fc * u + jnp.where(low8, sign * bc * swap(w), 0.0)
            d1 = jnp.where(low8, fc * w, (sign * THIRD) * swap(u))
            for o in range(8):
                c = 8 * b + o
                shift = lax.rem(start + 128 - COLS * o, 128)
                r1[1, c, 0:8, :] = r1[1, c, 0:8, :] + jnp.where(here, pltpu.roll(d0, shift, 1), 0.0)
                r1[1, c, 8:16, :] = r1[1, c, 8:16, :] + jnp.where(here, pltpu.roll(d1, shift, 1), 0.0)

    for side, c in ((0, 0), (1, LON - 1)):
        sign = 1.0 - 2.0 * side
        g = jnp.zeros((PIECE, 128), F32)
        for k in range(4):
            for t in range(2):
                for s in range(2):
                    m = 4 * k + 2 * t + s
                    g = g + ys[0, s, t, :, 4 * c + k : 4 * c + k + 1] * ww[side, m : m + 1, :]
        u = rotated(g[0:8], ww[side, 16:17, :], ww[side, 17:18, :])
        w = g[8:16]
        fc, bc = cw[side, 0], cw[side, 1]
        d0 = fc * u + jnp.where(low8, 0.0, sign * bc * w)
        d1 = jnp.where(low8, fc * w, (sign * THIRD) * u)
        r1[1, c, 0:8, :] = r1[1, c, 0:8, :] + jnp.where(own_lanes[side], d0, 0.0)
        r1[1, c, 8:16, :] = r1[1, c, 8:16, :] + jnp.where(own_lanes[side], d1, 0.0)

    phase_2(1)

    phase_3(0)
    pick_rows(1)
    phase_3(1)

    @pl.when(is_edge)
    def _():
        ghost_columns(0)
        sweep(0, second)

    start_halo(1)
    fill_halo(1)

    @pl.when(is_edge)
    def _():
        ghost_columns(1)

    def third(a, r, v):
        out[a, r] = to_state(a, r, v)

    sweep(1, third)

    take_bytes(hv_row, sem_hv.at[0])
    take_bytes(hv_col, sem_hv.at[3])
    take_bytes(metas.at[pl.ds(0, LON - 1)], sem_m.at[0])
    take_bytes(other_bases, sem_b.at[0])

    @pl.when(is_edge)
    def _():
        take_bytes(edges.at[pl.ds(0, LON - 1)], sem_c.at[0])

    for n in range(2):
        take_bytes(h_row.at[n], sem_h.at[n, 0])
        take_bytes(h_col.at[n], sem_h.at[n, 3])
        take_bytes(r1.at[n, pl.ds(0, LON - 1)], sem_1.at[n, 0])
        take_bytes(xb.at[n], sem_2.at[n, 0])
        take_bytes(r1.at[n, pl.ds(0, LAT - 2)], sem_2.at[n, 2])

        @pl.when(lat_edge)
        def _():
            take_bytes(dd.at[n, pl.ds(0, LON - 1)], sem_3.at[n, 0])

        @pl.when(jnp.logical_not(lat_edge))
        def _():
            @pl.when(lon_edge)
            def _():
                take_bytes(dd.at[n, 0], sem_3.at[n, 0])

            @pl.when(jnp.logical_not(lon_edge))
            def _():
                take_bytes(dd.at[n, pl.ds(0, 2)], sem_3.at[n, 0])


def body(viscosity, forcing, send_cell, partner, ghost_src, ghost_weight, ghost_angle):
    dma = pltpu.SemaphoreType.DMA

    def floats(*shape):
        return pltpu.VMEM(shape, F32)

    def ints(*shape):
        return pltpu.VMEM(shape, I32)

    scratch = [
        floats(ROWS, COLS, DEPTH),
        floats(4, ROWS, COLS, DEPTH),
        ints(8, 128),
        ints(1, 4),
        ints(1, GHOSTS),
        floats(1, GHOSTS),
        floats(4, GHOSTS),
        floats(ROWS + 2, C0 + COLS + 8, DEPTH),
        floats(2, COLS, DEPTH),
        floats(2, ROWS, DEPTH),
        floats(2, COLS, DEPTH),
        floats(2, ROWS, DEPTH),
        floats(2, 4, ROWS + 2, C0 + COLS + 8, DEPTH),
        floats(6, ROWS, COLS, DEPTH),
        floats(ROWS, COLS, DEPTH),
        floats(4, ROWS, COLS, DEPTH),
        floats(3, ROWS, COLS, DEPTH),
        floats(2, 2, 4, COLS, DEPTH),
        floats(2, 2, 4, ROWS, DEPTH),
        floats(2, 2, 4, COLS, DEPTH),
        floats(2, 2, 4, ROWS, DEPTH),
        ints(1, 128),
        ints(LON, 1, 128),
        ints(LON, 128),
        ints(1, 128),
        ints(LAT, 1, 128),
        ints(LAT, 128),
        floats(8, 128),
        floats(128, 128),
        floats(2, 4, CELLS, DEPTH),
        floats(2, LON * PIECE, CELLS),
        floats(2, LON, PIECE, CELLS),
        floats(LON, 4, 128),
        floats(LON, 4, 128),
        floats(2, LON, 128),
        floats(2, 2, 2, PIECE, 128),
        floats(2, PIECE, 128),
        floats(2, LAT, 2, PIECE, 128),
        floats(2, 2, 2, PIECE, 128),
        floats(2, LON, 4, 128),
        floats(2, LON, 4, 128),
        floats(256, 128),
        floats(4, GHOSTS, DEPTH),
        floats(72, 128),
        floats(2, 24, 128),
        floats(2, 4, 8, 128),
        floats(2, 2, 8, 128),
        dma((7,)), dma((4,)), dma((2,)), dma((2,)), dma((2, 4)), dma((2, 2)), dma((2,)),
        dma((2, 3)), dma((2, 2)), pltpu.SemaphoreType.REGULAR,
    ]
    state = pl.pallas_call(
        kernel,
        out_shape=jax.ShapeDtypeStruct((4, ROWS, COLS, DEPTH), F32),
        in_specs=[pl.BlockSpec(memory_space=pl.ANY)] * 7,
        out_specs=pl.BlockSpec(memory_space=pltpu.VMEM),
        scratch_shapes=scratch,
        compiler_params=pltpu.CompilerParams(
            collective_id=0, has_side_effects=True, vmem_limit_bytes=63 << 20
        ),
    )(
        viscosity.reshape(ROWS, COLS, DEPTH),
        forcing.reshape(4, ROWS, COLS, DEPTH),
        send_cell.reshape(LAT, 4 * LON),
        partner.reshape(1, 4),
        ghost_src.reshape(1, GHOSTS),
        ghost_angle.reshape(1, GHOSTS),
        jnp.swapaxes(ghost_weight, 3, 4).reshape(4, GHOSTS),
    )
    return state[:, None]


def solution(mesh):
    placed = (
        P("panel", "lat", "lon", None),
        P(None, "panel", "lat", "lon", None),
        P("panel", "lat", "lon", None),
        P("panel", "lat", "lon", None),
        P("panel", "lat", "lon", None),
        P("panel", "lat", "lon", None, None),
        P("panel", "lat", "lon", None),
    )
    return jax.shard_map(
        body,
        mesh=mesh,
        in_specs=placed,
        out_specs=P(None, "panel", "lat", "lon", None),
        check_vma=False,
    )
```
